32 devices in a mesh: tile: 4 (over y, x), depth: 8 (over z, core).
Axes of the slice: x: 2, y: 2, z: 4, core: 2. Of those that a mesh axis runs over, the one named last changes fastest.
Arguments:
- volume: bfloat16 [4, 8, 128, 128, 128], P('tile', 'depth'), may hold values from -8 to 8
- shear: float32 [4, 8, 2], P('tile', 'depth'), may hold values from -0.5 to 0.5
- absorb: float32 [4, 8], P('tile', 'depth'), may hold values from 0.000390625 to 0.0078125
- color_slope: float32 [3], replicated, may hold values from -3 to 3
- color_bias: float32 [3], replicated, may hold values from -1.5 to 1.5
- frag_tile: int32 [4, 8, 16, 1], P('tile', 'depth'), may hold values from 0 to 3; in each aligned block of 16 rows (0 to 15, 16 to 31, ..., all dimensions but the last counted through in order) at most 4 rows name the same one
- slot_perm: int32 [4, 8, 4, 16], P('tile', 'depth'), may hold values from 0 to 15, each once within a row
- frag_rows: int32 [4, 8, 16], P('tile', 'depth'), may hold values from 1 to 64
- tile_view: int32 [4], replicated, may hold values from 0 to 1
- tile_owner: int32 [4], replicated, may hold values from 0 to 3, each once
Outputs:
- frame: bfloat16 [4, 4, 256, 256], P('tile')
The draws below stay inside these ranges and needn't reach their ends.
Inputs may be any that keep to these rules, and one draw needn't show every extreme that they name: `frag_tile`: each brick puts at most 4 fragments on one screen tile, and some brick puts exactly 4 there in every draw. `slot_perm`: each row is a permutation of the positions. `tile_owner`: A permutation of the tiles.
All inputs are finite; a program needn't handle non-finite values.
Results may differ from the reference program's by a relative error of at most 0.0035.
Values may be sent and summed in bfloat16 or wider, within the bound.
A program may use at most 64 MiB of HBM per device.

```python
import math
import jax
import jax.numpy as jnp
import numpy as np
from jax import lax

BRICK = 128
SAMPLES = 128
RAYS = 256
FRAG = 64
TILE_SIDE = 256
CAP = 4
FRAGS = 16
POS = 16
TILES = 4
SLABS = 8


def shared_view(key):
    shear_key = jax.random.fold_in(key, 7101)
    return jax.random.uniform(shear_key, (TILES, SLABS, 2), jnp.float32, -0.5, 0.5)


def draw_shear(key, part):
    return shared_view(key)


def draw_volume(key, part):
    shear_now = shared_view(key)
    frequency = jax.random.uniform(jax.random.fold_in(key, 7102), (TILES, SLABS, 2), jnp.float32, 0.8 * math.pi, 0.92 * math.pi)
    offset_angle = jax.random.uniform(jax.random.fold_in(key, 7103), (TILES, SLABS, 2), jnp.float32, -math.pi, math.pi)
    cell_pos = jnp.arange(BRICK).astype(jnp.float32)
    centred = cell_pos - (BRICK - 1) / 2.0
    row_shift = shear_now[:, :, 0][:, :, None] * centred[None, None, :]
    col_shift = shear_now[:, :, 1][:, :, None] * centred[None, None, :]
    row_wave = jnp.cos(frequency[:, :, 0][:, :, None, None] * (cell_pos[None, None, None, :] - row_shift[:, :, :, None]) + offset_angle[:, :, 0][:, :, None, None])
    col_wave = jnp.cos(frequency[:, :, 1][:, :, None, None] * (cell_pos[None, None, None, :] - col_shift[:, :, :, None]) + offset_angle[:, :, 1][:, :, None, None])
    jitter_key = jax.random.fold_in(key, 7104)
    full_shape = (TILES, SLABS, BRICK, BRICK, BRICK)
    jitter = 2.0 * jax.random.normal(jitter_key, full_shape, jnp.float32)
    volume = jitter + 3.0 * row_wave[:, :, :, :, None] + 3.0 * col_wave[:, :, :, None, :]
    return jnp.clip(volume, -8.0, 8.0).astype(jnp.bfloat16)


def plant(result, stream_key, smallest, top_value):
    longest = result.shape.index(max(result.shape))
    spots = []
    for shift in (0, 1):
        where = [jax.random.randint(jax.random.fold_in(stream_key, axis), (), 0, length) for axis, length in enumerate(result.shape)]
        where[longest] = (where[longest] + shift) % result.shape[longest]
        spots.append(tuple(where))
    return result.at[spots[0]].set(smallest).at[spots[1]].set(top_value)


def level_of(rng, extent, shards, least, high):
    level, own = 1.0, jax.random.fold_in(rng, 6)
    for axis_at, blocks in shards:
        heights = jnp.exp(jax.random.uniform(jax.random.fold_in(own, axis_at), (blocks,), jnp.float32, least / len(shards), high / len(shards)))
        level = level * jnp.repeat(heights, extent[axis_at] // blocks).reshape([-1 if axis == axis_at else 1 for axis in range(len(extent))])
    return level


def deal_out(own_key, own, number, rows, count, top, reach, slope):
    order = jax.random.permutation(own_key, count)
    heavy_load, ordinary = portions_of(count, rows * top, reach, slope, True), portions_of(count, rows * top, reach, slope, False)
    places = jnp.arange(count)

    def named(lengths, turn):
        used = int((lengths > 0).sum())
        fixed = max(1, used // 4)
        moved = fixed + (places - fixed + turn * (used - fixed)) % max(1, count - fixed)
        return jnp.zeros((count,), jnp.int32).at[order[jnp.where(places < fixed, places, moved)]].set(jnp.asarray(lengths, jnp.int32))

    lengths = jnp.where(number % 4 == 0, named(heavy_load, number // 4), named(ordinary, number - number // 4 - 1))
    mixed = jax.random.permutation(jax.random.fold_in(own, 3), count)
    giver, receiver = mixed[0:count // 2 * 2:2], mixed[1:count // 2 * 2:2]
    slack = jnp.minimum(lengths[giver] - 1, reach - lengths[receiver]) // 2
    slack = jnp.where((giver == order[0]) | (receiver == order[0]) | (lengths[receiver] == 0), 0, jnp.maximum(slack, 0))
    moved = jax.random.randint(jax.random.fold_in(own, 4), (count // 2,), 0, 1 << 20) % (slack + 1)
    lengths = lengths.at[giver].add(-moved).at[receiver].add(moved)
    labels = jnp.searchsorted(jnp.cumsum(lengths), jnp.arange(rows * top), side="right").astype(jnp.int32)
    table = labels.reshape(top, rows).T
    table = table[jax.random.permutation(jax.random.fold_in(own, 1), rows)]
    turn = jax.random.randint(jax.random.fold_in(own, 2), (rows, 1), 0, top)
    return jnp.take_along_axis(table, (jnp.arange(top)[None, :] + turn) % top, axis=1)


def portions_of(amount, total, limit, lean, full):
    portions = [(1 << 20) // math.isqrt(standing ** lean) + 1 for standing in range(1, amount + 1)]
    largest = limit if full else min(limit, max(-(-total // amount), total * portions[0] // sum(portions)))
    least = 1 if total - largest >= amount - 1 else 0
    holding, surplus = [largest] + [least] * (amount - 1), total - largest - least * (amount - 1)
    while surplus > 0:
        movable = [i for i in range(1, amount) if holding[i] < largest] or [i for i in range(1, amount) if holding[i] < limit]
        whole, remaining = sum([portions[i] for i in movable]), surplus
        for i in movable:
            extra = min(limit - holding[i], max(1, remaining * portions[i] // whole), surplus)
            holding[i] = holding[i] + extra
            surplus = surplus - extra
    return np.array(holding)


def setup_inputs(seed: int = 0) -> dict:
    seeds = jax.random.split(jax.random.key(seed), 11)
    volume = draw_volume(jax.random.fold_in(seeds[10], 71), 0)
    shear = draw_shear(jax.random.fold_in(seeds[10], 71), 0)
    absorb = jnp.clip(jnp.exp(math.log(0.0078125) - 2.9957323 * jax.random.uniform(seeds[2], (TILES, SLABS), jnp.float32) ** level_of(seeds[2], (TILES, SLABS), ((0, 4), (1, 8)), -0.2, 0.2)), 0.000390625, 0.0078125)
    color_slope = jnp.clip(jax.random.uniform(seeds[3], (3,), jnp.float32, -3.0, 3.0), -3.0, 3.0)
    color_bias = jnp.clip(jax.random.uniform(seeds[4], (3,), jnp.float32, -1.5, 1.5), -1.5, 1.5)
    frag_tile_keys = jax.random.split(jax.random.fold_in(seeds[5], 1), TILES * SLABS * FRAGS // FRAGS)
    frag_tile_turns = jax.random.permutation(jax.random.fold_in(seeds[5], 3), TILES * SLABS * FRAGS // FRAGS)
    frag_tile = jax.vmap(lambda own, number: deal_out(jax.random.fold_in(seeds[5], 2), own, number, FRAGS, TILES, 1, CAP, 2))(frag_tile_keys, frag_tile_turns).reshape((TILES, SLABS, FRAGS, 1))
    slot_perm = jax.vmap(lambda own: jax.random.permutation(own, POS))(jax.random.split(seeds[6], TILES * SLABS * TILES)).reshape((TILES, SLABS, TILES, POS)).astype(jnp.int32)
    frag_rows = plant(jax.random.randint(seeds[7], (TILES, SLABS, FRAGS), 1, FRAG + 1), jax.random.fold_in(seeds[7], 1), 1, FRAG).astype(jnp.int32)
    tile_view = plant(jax.random.randint(seeds[8], (TILES,), 0, 2), jax.random.fold_in(seeds[8], 1), 0, 1).astype(jnp.int32)
    tile_owner = jax.random.permutation(seeds[9], TILES).astype(jnp.int32)
    return {"volume": volume, "shear": shear, "absorb": absorb, "color_slope": color_slope, "color_bias": color_bias, "frag_tile": frag_tile, "slot_perm": slot_perm, "frag_rows": frag_rows, "tile_view": tile_view, "tile_owner": tile_owner}


def spline(offset):
    size_abs = jnp.abs(offset)
    inner = 2.0 / 3.0 - size_abs * size_abs + 0.5 * size_abs * size_abs * size_abs
    remain = 2.0 - size_abs
    outer = remain * remain * remain / 6.0
    return jnp.where(size_abs < 1.0, inner, jnp.where(size_abs < 2.0, outer, 0.0))


def tables(shear_pair, sample_index, side, rays, samples):
    cells = jnp.arange(side).astype(jnp.float32)
    depth_pos = (sample_index.astype(jnp.float32) + 0.5) * side / samples - 0.5
    ray_pos = (jnp.arange(rays).astype(jnp.float32) + 0.5) * side / rays - 0.5
    centred = depth_pos - (side - 1) / 2.0
    depth_table = spline(depth_pos[:, None] - cells[None, :])
    row_pos = ray_pos[None, :] + shear_pair[0] * centred[:, None]
    col_pos = ray_pos[None, :] + shear_pair[1] * centred[:, None]
    row_table = spline(row_pos[:, :, None] - cells[None, None, :])
    col_table = spline(col_pos[:, :, None] - cells[None, None, :])
    return depth_table.astype(jnp.bfloat16), row_table.astype(jnp.bfloat16), col_table.astype(jnp.bfloat16)


def render(brick, shear_pair, rate, color_slope, color_bias):
    side = brick.shape[0]
    sample_index = jnp.arange(SAMPLES, dtype=jnp.int32)
    depth_table, row_table, col_table = tables(shear_pair, sample_index, side, RAYS, SAMPLES)
    resampled = jnp.dot(depth_table, brick.reshape(side, side * side), preferred_element_type=jnp.float32)
    resampled = resampled.astype(jnp.bfloat16).reshape(SAMPLES, side, side)
    half_way = jnp.einsum("sua,sab->sub", row_table.astype(jnp.float32), resampled.astype(jnp.float32), precision=lax.Precision.HIGHEST).astype(jnp.bfloat16)
    field = jnp.einsum("sub,svb->suv", half_way.astype(jnp.float32), col_table.astype(jnp.float32), precision=lax.Precision.HIGHEST)
    softness = jax.nn.softplus(field)
    before = jnp.cumsum(softness, 0) - softness
    weight = jnp.exp(-rate * before) * (1.0 - jnp.exp(-rate * softness))
    colors = [jnp.sum(weight * jax.nn.sigmoid(color_slope[k] * field + color_bias[k]), 0) for k in range(3)]
    alpha = 1.0 - jnp.exp(-rate * jnp.sum(softness, 0))
    return jnp.stack(colors + [alpha]).astype(jnp.bfloat16)


def reference(volume, shear, absorb, color_slope, color_bias, frag_tile, slot_perm, frag_rows, tile_view, tile_owner):
    tiles = volume.shape[0]
    slabs = volume.shape[1]
    side = volume.shape[2]
    bricks = volume.reshape(tiles * slabs, side, side, side)
    shears = shear.reshape(tiles * slabs, 2)
    rates = absorb.reshape(tiles * slabs)
    images = lax.map(lambda item: render(item[0], item[1], item[2], color_slope, color_bias), (bricks, shears, rates))
    per_side = RAYS // FRAG
    frags = images.reshape(tiles, slabs, 4, per_side, FRAG, per_side, FRAG)
    frags = frags.transpose(0, 1, 3, 5, 2, 4, 6).reshape(tiles, slabs, per_side * per_side, 4, FRAG, FRAG)
    keep = jnp.arange(FRAG)[None, None, None, :] < frag_rows[:, :, :, None]
    frags = frags.astype(jnp.float32) * keep[:, :, :, None, :, None].astype(jnp.float32)
    target = frag_tile[:, :, :, 0]
    onehot = (target[..., None] == jnp.arange(tiles)[None, None, None, :]).astype(jnp.int32)
    rank = jnp.sum((jnp.cumsum(onehot, 2) - onehot) * onehot, -1).astype(jnp.int32)
    by_tile = jnp.take_along_axis(slot_perm, target[..., None].astype(jnp.int32), axis=2)
    position = jnp.take_along_axis(by_tile, rank[..., None], axis=3)[..., 0].astype(jnp.int32)
    slab_index = jnp.broadcast_to(jnp.arange(slabs, dtype=jnp.int32)[None, :, None], target.shape)
    layer = jnp.zeros((slabs, tiles, POS, 4, FRAG, FRAG), jnp.float32)
    layer = layer.at[slab_index, target, position].add(frags)
    flipped = tile_view[None, :, None, None, None, None] == 1
    ordered = jnp.where(flipped, layer[::-1], layer)
    clear = 1.0 - ordered[:, :, :, 3]
    running = jnp.cumprod(clear, 0)
    infront = jnp.concatenate([jnp.ones_like(running[:1]), running[:-1]], 0)
    color = jnp.sum(infront[:, :, :, None] * ordered[:, :, :, :3], 0)
    alpha = 1.0 - running[-1]
    composite = jnp.concatenate([color, alpha[:, :, None]], 2)
    per_tile = TILE_SIDE // FRAG
    composite = composite.reshape(tiles, per_tile, per_tile, 4, FRAG, FRAG).transpose(0, 3, 1, 4, 2, 5)
    composite = composite.reshape(tiles, 4, TILE_SIDE, TILE_SIDE).astype(jnp.bfloat16)
    return jnp.zeros_like(composite).at[tile_owner].set(composite)
```

```python
import functools
import jax
import jax.numpy as jnp
from jax import lax
from jax.experimental import pallas as pl
from jax.experimental.pallas import tpu as pltpu
from jax.sharding import PartitionSpec as P

SAMPLES = 128
RAYS = 256
FRAG = 64
TILE_SIDE = 256
CAP = 4
POS = 16
GROUP = 4
ROWS = 16
TAPS = 4
LOG2E = 1.4426950408889634


def spline(offset):
    size_abs = jnp.abs(offset)
    inner = 2.0 / 3.0 - size_abs * size_abs + 0.5 * size_abs * size_abs * size_abs
    remain = 2.0 - size_abs
    outer = remain * remain * remain / 6.0
    return jnp.where(size_abs < 1.0, inner, jnp.where(size_abs < 2.0, outer, 0.0))


def taps_of(shear_one, side):
    per = RAYS // side
    centred = jnp.arange(SAMPLES).astype(jnp.float32) - (side - 1) / 2.0
    base = (jnp.arange(per).astype(jnp.float32) + 0.5) / per - 0.5
    place = base[None, :] + shear_one * centred[:, None]
    whole = jnp.floor(place)
    part = place - whole
    reach = jnp.arange(TAPS).astype(jnp.float32) - 1.0
    weight = spline(part[:, :, None] - reach)
    weight = weight.astype(jnp.bfloat16).astype(jnp.float32)
    cell = whole[:, :, None] + reach
    return jnp.concatenate([weight, cell], 2).reshape(SAMPLES * per * 2 * TAPS)


def band(taps, at, offsets, odd):
    def value(index):
        even_one = taps[at + index]
        odd_one = taps[at + 2 * TAPS + index]
        return jnp.where(odd, odd_one, even_one).astype(jnp.bfloat16)

    result = jnp.zeros(offsets.shape, jnp.bfloat16)
    for tap in range(TAPS):
        result = jnp.where(offsets == value(TAPS + tap)[None], value(tap)[None], result)
    return result


def render_kernel(
    volume, row_taps, col_taps, scalars, rows_live, image, row_off, col_off, field_a, field_b, state
):
    side = volume.shape[0]
    per = RAYS // side
    first = jnp.float32(jnp.bfloat16(2.0 / 3.0))
    second = jnp.float32(jnp.bfloat16(1.0 / 6.0))
    rate = scalars[0]
    slope = [scalars[1 + k] * 0.5 for k in range(3)]
    bias = [scalars[4 + k] * 0.5 for k in range(3)]

    row_shape = (RAYS // 16, 16, side)
    ray = lax.broadcasted_iota(jnp.int32, row_shape, 0) * 16 + lax.broadcasted_iota(
        jnp.int32, row_shape, 1
    )
    cell = lax.broadcasted_iota(jnp.int32, row_shape, 2)
    row_off[...] = (cell - ray // per).astype(jnp.float32).astype(jnp.bfloat16)
    col_shape = (side // 16, 16, RAYS)
    cell = lax.broadcasted_iota(jnp.int32, col_shape, 0) * 16 + lax.broadcasted_iota(
        jnp.int32, col_shape, 1
    )
    ray = lax.broadcasted_iota(jnp.int32, col_shape, 2)
    col_off[...] = (cell - ray // per).astype(jnp.float32).astype(jnp.bfloat16)
    row_odd = lax.broadcasted_iota(jnp.int32, (16, side), 0) % per == 1
    col_odd = lax.broadcasted_iota(jnp.int32, (16, RAYS), 1) % per == 1

    state[0] = jnp.ones((RAYS, RAYS), jnp.float32)
    for k in range(3):
        state[1 + k] = jnp.zeros((RAYS, RAYS), jnp.float32)

    def fields(start, out):
        last = SAMPLES - 1
        slices = [
            volume[jnp.clip(start + j - 1, 0, last)].astype(jnp.float32) for j in range(GROUP + 2)
        ]
        for j in range(GROUP):
            sample = jnp.minimum(start + j, last)
            below = jnp.where(sample == 0, 0.0, second)
            above = jnp.where(sample == last, 0.0, second)
            part = slices[j] * below + slices[j + 1] * first + slices[j + 2] * above
            part = part.astype(jnp.bfloat16)
            at = sample * (per * 2 * TAPS)
            row_table = band(row_taps, at, row_off[...], row_odd).reshape(RAYS, side)
            col_table = band(col_taps, at, col_off[...], col_odd).reshape(side, RAYS)
            half_way = jnp.dot(row_table, part, preferred_element_type=jnp.float32)
            out[j] = jnp.dot(
                half_way.astype(jnp.bfloat16), col_table, preferred_element_type=jnp.float32
            )

    def integrate(source):
        for tile in range(RAYS // ROWS):
            rows = slice(tile * ROWS, (tile + 1) * ROWS)
            clear = state[0, rows]
            colors = [state[1 + k, rows] for k in range(3)]
            for j in range(GROUP):
                field = source[j, rows]
                soft = jnp.log2(1.0 + jnp.exp2(field * LOG2E))
                after = clear * jnp.exp2(soft * -rate)
                weight = clear - after
                clear = after
                colors = [
                    colors[k] + weight * jnp.tanh(field * slope[k] + bias[k]) for k in range(3)
                ]
            state[0, rows] = clear
            for k in range(3):
                state[1 + k, rows] = colors[k]

    fields(0, field_a)

    def step(index, carry):
        start = index * (2 * GROUP)
        fields(start + GROUP, field_b)
        integrate(field_a)
        fields(start + 2 * GROUP, field_a)
        integrate(field_b)
        return carry

    lax.fori_loop(0, SAMPLES // (2 * GROUP), step, 0)

    per_side = RAYS // FRAG
    row = lax.broadcasted_iota(jnp.int32, (FRAG, RAYS), 0)
    lane = lax.broadcasted_iota(jnp.int32, (FRAG, RAYS), 1)
    for fu in range(per_side):
        live = jnp.zeros((FRAG, RAYS), jnp.int32)
        for fv in range(per_side):
            live = jnp.where(lane // FRAG == fv, rows_live[fu * per_side + fv], live)
        keep = row < live
        rows = slice(fu * FRAG, (fu + 1) * FRAG)
        alpha = 1.0 - state[0, rows]
        for k in range(3):
            color = 0.5 * (alpha + state[1 + k, rows])
            image[k, rows] = jnp.where(keep, color, 0.0).astype(jnp.bfloat16)
        image[3, rows] = jnp.where(keep, alpha, 0.0).astype(jnp.bfloat16)


def render(brick, shear_pair, rate, color_slope, color_bias, rows_live):
    side = brick.shape[0]
    smem = pl.BlockSpec(memory_space=pltpu.SMEM)
    vmem = pl.BlockSpec(memory_space=pltpu.VMEM)
    scalars = jnp.concatenate([rate[None], color_slope, color_bias, jnp.zeros((1,), jnp.float32)])
    return pl.pallas_call(
        render_kernel,
        out_shape=jax.ShapeDtypeStruct((4, RAYS, RAYS), jnp.bfloat16),
        in_specs=[vmem, smem, smem, smem, smem],
        out_specs=vmem,
        scratch_shapes=[
            pltpu.VMEM((RAYS // 16, 16, side), jnp.bfloat16),
            pltpu.VMEM((side // 16, 16, RAYS), jnp.bfloat16),
            pltpu.VMEM((GROUP, RAYS, RAYS), jnp.float32),
            pltpu.VMEM((GROUP, RAYS, RAYS), jnp.float32),
            pltpu.VMEM((4, RAYS, RAYS), jnp.float32),
        ],
        compiler_params=pltpu.CompilerParams(vmem_limit_bytes=32 * 2**20),
        cost_estimate=pl.CostEstimate(
            flops=2 * SAMPLES * RAYS * side * (side + RAYS),
            bytes_accessed=brick.size * 2,
            transcendentals=6 * SAMPLES * RAYS * RAYS,
        ),
        name="render",
    )(brick, taps_of(shear_pair[0], side), taps_of(shear_pair[1], side), scalars, rows_live)


def swapped(value, axis, apart):
    mask = 2**apart
    pairs = [(source, source ^ mask) for source in range(lax.axis_size(axis))]
    return lax.ppermute(value, axis, pairs)


def over(front, back):
    veil = 1.0 - front[3:4]
    return jnp.concatenate([front[:3] + veil * back[:3], front[3:4] + veil * back[3:4]], 0)


def local(
    volume,
    shear,
    absorb,
    color_slope,
    color_bias,
    frag_tile,
    slot_perm,
    frag_rows,
    tile_view,
    tile_owner,
):
    image = render(volume[0, 0], shear[0, 0], absorb[0, 0], color_slope, color_bias, frag_rows[0, 0])
    per_side = RAYS // FRAG
    count = per_side * per_side
    frags = image.reshape(4, per_side, FRAG, per_side, FRAG).transpose(1, 3, 0, 2, 4)
    frags = frags.reshape(count, 4 * FRAG * FRAG)
    group_size = lax.axis_size("tile")
    column = lax.axis_index("tile")
    target = frag_tile[0, 0, :, 0]
    onehot = (target[:, None] == jnp.arange(group_size)[None, :]).astype(jnp.int32)
    rank = jnp.sum((jnp.cumsum(onehot, 0) - onehot) * onehot, 1)
    row_perm = jnp.sum(onehot[:, :, None] * slot_perm[0, 0][None], 1)
    position = jnp.sum(row_perm * (rank[:, None] == jnp.arange(POS)[None, :]).astype(jnp.int32), 1)
    receiver = jnp.sum(onehot * tile_owner[None, :], 1)
    to_peer = receiver[:, None] == jnp.arange(group_size)[None, :]
    select = to_peer[:, :, None] & (rank[:, None, None] == jnp.arange(CAP)[None, None, :])
    select = select.reshape(count, group_size * CAP).T.astype(jnp.bfloat16)
    outgoing = jnp.dot(select, frags, preferred_element_type=jnp.float32).astype(jnp.bfloat16)
    incoming = lax.all_to_all(
        outgoing.reshape(group_size, CAP, 4 * FRAG * FRAG),
        "tile",
        split_axis=0,
        concat_axis=0,
        tiled=True,
    )
    all_receiver, all_rank, all_position = (
        lax.all_gather(receiver, "tile", axis=0, tiled=True),
        lax.all_gather(rank, "tile", axis=0, tiled=True),
        lax.all_gather(position, "tile", axis=0, tiled=True),
    )
    mine = (all_receiver == column).reshape(group_size, count)
    at_place = (
        all_position.reshape(group_size, count)[:, :, None] == jnp.arange(POS)[None, None, :]
    ) & mine[:, :, None]
    at_slot = all_rank.reshape(group_size, count)[:, :, None] == jnp.arange(CAP)[None, None, :]
    place = jnp.einsum("sfp,sfk->psk", at_place.astype(jnp.float32), at_slot.astype(jnp.float32))
    place = place.reshape(POS, group_size * CAP).astype(jnp.bfloat16)
    layer = jnp.dot(
        place,
        incoming.reshape(group_size * CAP, 4 * FRAG * FRAG),
        preferred_element_type=jnp.float32,
    )
    per_tile = TILE_SIDE // FRAG
    tile_image = (
        layer.reshape(per_tile, per_tile, 4, FRAG, FRAG)
        .transpose(2, 0, 3, 1, 4)
        .reshape(4, TILE_SIDE, TILE_SIDE)
    )
    my_view = jnp.sum(jnp.where(tile_owner == column, tile_view, 0))
    slab_count = lax.axis_size("depth")
    slab_index = lax.axis_index("depth")
    strip_rows = TILE_SIDE // slab_count
    current = tile_image.reshape(4, slab_count, strip_rows, TILE_SIDE)
    for level in range(slab_count.bit_length() - 1):
        width_now = current.shape[1]
        paired = current.reshape(4, width_now // 2, 2, strip_rows, TILE_SIDE)
        even_part = paired[:, :, 0]
        odd_part = paired[:, :, 1]
        upper = jnp.right_shift(slab_index, level) % 2 == 1
        kept = jnp.where(upper, odd_part, even_part)
        given = jnp.where(upper, even_part, odd_part)
        other = swapped(given.astype(jnp.bfloat16), "depth", level).astype(jnp.float32)
        mine_front = jnp.logical_not(upper) != (my_view == 1)
        current = over(jnp.where(mine_front, kept, other), jnp.where(mine_front, other, kept))
    strip = current.reshape(4, strip_rows, TILE_SIDE)
    finished = lax.all_gather(strip.astype(jnp.bfloat16), "depth", axis=1, tiled=True)
    return finished[None]


def solution(mesh):
    in_specs = (
        P("tile", "depth", None, None, None),
        P("tile", "depth", None),
        P("tile", "depth"),
        P(),
        P(),
        P("tile", "depth", None, None),
        P("tile", "depth", None, None),
        P("tile", "depth", None),
        P(),
        P(),
    )
    out_specs = P("tile", None, None, None)
    return jax.shard_map(local, mesh=mesh, in_specs=in_specs, out_specs=out_specs, check_vma=False)
```

```python
import functools
import jax
import jax.numpy as jnp
from jax import lax
from jax.experimental import pallas as pl
from jax.experimental.pallas import tpu as pltpu
from jax.sharding import PartitionSpec as P

SAMPLES = 128
RAYS = 256
FRAG = 64
TILE_SIDE = 256
CAP = 4
POS = 16
GROUP = 4
ROWS = 16
TAPS = 4
LOG2E = 1.4426950408889634


def spline(offset):
    size_abs = jnp.abs(offset)
    inner = 2.0 / 3.0 - size_abs * size_abs + 0.5 * size_abs * size_abs * size_abs
    remain = 2.0 - size_abs
    outer = remain * remain * remain / 6.0
    return jnp.where(size_abs < 1.0, inner, jnp.where(size_abs < 2.0, outer, 0.0))


def taps_of(shear_one, side):
    per = RAYS // side
    centred = jnp.arange(SAMPLES).astype(jnp.float32) - (side - 1) / 2.0
    base = (jnp.arange(per).astype(jnp.float32) + 0.5) / per - 0.5
    place = base[None, :] + shear_one * centred[:, None]
    whole = jnp.floor(place)
    part = place - whole
    reach = jnp.arange(TAPS).astype(jnp.float32) - 1.0
    weight = spline(part[:, :, None] - reach)
    weight = weight.astype(jnp.bfloat16).astype(jnp.float32)
    cell = whole[:, :, None] + reach
    return jnp.concatenate([weight, cell], 2).reshape(SAMPLES * per * 2 * TAPS)


def band(taps, at, offsets, odd):
    def value(index):
        even_one = taps[at + index]
        odd_one = taps[at + 2 * TAPS + index]
        return jnp.where(odd, odd_one, even_one).astype(jnp.bfloat16)

    result = jnp.zeros(offsets.shape, jnp.bfloat16)
    for tap in range(TAPS):
        result = jnp.where(offsets == value(TAPS + tap)[None], value(tap)[None], result)
    return result


def render_kernel(
    volume,
    row_taps,
    col_taps,
    scalars,
    rows_live,
    target,
    perm,
    owner,
    outgoing,
    slots,
    row_off,
    col_off,
    field_a,
    field_b,
    state,
    dealt,
    place,
):
    side = volume.shape[0]
    per = RAYS // side
    first = jnp.float32(jnp.bfloat16(2.0 / 3.0))
    second = jnp.float32(jnp.bfloat16(1.0 / 6.0))
    rate = scalars[0]
    slope = [scalars[1 + k] * 0.5 for k in range(3)]
    bias = [scalars[4 + k] * 0.5 for k in range(3)]

    row_shape = (RAYS // 16, 16, side)
    ray = lax.broadcasted_iota(jnp.int32, row_shape, 0) * 16 + lax.broadcasted_iota(
        jnp.int32, row_shape, 1
    )
    cell = lax.broadcasted_iota(jnp.int32, row_shape, 2)
    row_off[...] = (cell - ray // per).astype(jnp.float32).astype(jnp.bfloat16)
    col_shape = (side // 16, 16, RAYS)
    cell = lax.broadcasted_iota(jnp.int32, col_shape, 0) * 16 + lax.broadcasted_iota(
        jnp.int32, col_shape, 1
    )
    ray = lax.broadcasted_iota(jnp.int32, col_shape, 2)
    col_off[...] = (cell - ray // per).astype(jnp.float32).astype(jnp.bfloat16)
    row_odd = lax.broadcasted_iota(jnp.int32, (16, side), 0) % per == 1
    col_odd = lax.broadcasted_iota(jnp.int32, (16, RAYS), 1) % per == 1

    state[0] = jnp.ones((RAYS, RAYS), jnp.float32)
    for k in range(3):
        state[1 + k] = jnp.zeros((RAYS, RAYS), jnp.float32)

    def fields(start, out):
        last = SAMPLES - 1
        slices = [
            volume[jnp.clip(start + j - 1, 0, last)].astype(jnp.float32) for j in range(GROUP + 2)
        ]
        for j in range(GROUP):
            sample = jnp.minimum(start + j, last)
            below = jnp.where(sample == 0, 0.0, second)
            above = jnp.where(sample == last, 0.0, second)
            part = slices[j] * below + slices[j + 1] * first + slices[j + 2] * above
            part = part.astype(jnp.bfloat16)
            at = sample * (per * 2 * TAPS)
            row_table = band(row_taps, at, row_off[...], row_odd).reshape(RAYS, side)
            col_table = band(col_taps, at, col_off[...], col_odd).reshape(side, RAYS)
            half_way = jnp.dot(row_table, part, preferred_element_type=jnp.float32)
            out[j] = jnp.dot(
                half_way.astype(jnp.bfloat16), col_table, preferred_element_type=jnp.float32
            )

    def integrate(source):
        for tile in range(RAYS // ROWS):
            rows = slice(tile * ROWS, (tile + 1) * ROWS)
            clear = state[0, rows]
            colors = [state[1 + k, rows] for k in range(3)]
            for j in range(GROUP):
                field = source[j, rows]
                soft = jnp.log2(1.0 + jnp.exp2(field * LOG2E))
                after = clear * jnp.exp2(soft * -rate)
                weight = clear - after
                clear = after
                colors = [
                    colors[k] + weight * jnp.tanh(field * slope[k] + bias[k]) for k in range(3)
                ]
            state[0, rows] = clear
            for k in range(3):
                state[1 + k, rows] = colors[k]

    fields(0, field_a)

    def step(index, carry):
        start = index * (2 * GROUP)
        fields(start + GROUP, field_b)
        integrate(field_a)
        fields(start + 2 * GROUP, field_a)
        integrate(field_b)
        return carry

    lax.fori_loop(0, SAMPLES // (2 * GROUP), step, 0)

    groups = owner.shape[0]
    per_side = RAYS // FRAG
    count = per_side * per_side
    for t in range(groups):
        dealt[t] = 0
        for p in range(POS):
            slots[t, 0, p] = -1
    for f in range(count):
        tile = target[f]
        rank = dealt[tile]
        dealt[tile] = rank + 1
        receiver = owner[tile]
        slots[receiver, 0, perm[tile * POS + rank]] = rank
        place[f] = receiver * CAP + rank
    if groups * CAP > count:
        outgoing[...] = jnp.zeros(outgoing.shape, outgoing.dtype)

    row = lax.broadcasted_iota(jnp.int32, (FRAG, 2 * FRAG), 0)
    low = lax.broadcasted_iota(jnp.int32, (FRAG, 2 * FRAG), 1) < FRAG
    for fu in range(per_side):
        for pair in range(per_side // 2):
            f = fu * per_side + 2 * pair
            keep = row < jnp.where(low, rows_live[f], rows_live[f + 1])
            rows = slice(fu * FRAG, (fu + 1) * FRAG)
            lanes = slice(pair * 2 * FRAG, (pair + 1) * 2 * FRAG)
            alpha = 1.0 - state[0, rows, lanes]
            parts = [0.5 * (alpha + state[1 + k, rows, lanes]) for k in range(3)] + [alpha]
            parts = [jnp.where(keep, part, 0.0) for part in parts]
            turned = [pltpu.roll(part, FRAG, 1) for part in parts]
            for c in range(2):
                even = jnp.where(low, parts[2 * c], turned[2 * c + 1])
                odd = jnp.where(low, turned[2 * c], parts[2 * c + 1])
                outgoing[place[f], c] = even.astype(jnp.bfloat16)
                outgoing[place[f + 1], c] = odd.astype(jnp.bfloat16)


def render(brick, shear_pair, rate, color_slope, color_bias, rows_live, target, perm, owner):
    side = brick.shape[0]
    groups = owner.shape[0]
    smem = pl.BlockSpec(memory_space=pltpu.SMEM)
    vmem = pl.BlockSpec(memory_space=pltpu.VMEM)
    scalars = jnp.concatenate([rate[None], color_slope, color_bias, jnp.zeros((1,), jnp.float32)])
    return pl.pallas_call(
        render_kernel,
        out_shape=(
            jax.ShapeDtypeStruct((groups * CAP, 2, FRAG, 2 * FRAG), jnp.bfloat16),
            jax.ShapeDtypeStruct((groups, 8, 128), jnp.int32),
        ),
        in_specs=[vmem] + [smem] * 7,
        out_specs=(vmem, smem),
        scratch_shapes=[
            pltpu.VMEM((RAYS // 16, 16, side), jnp.bfloat16),
            pltpu.VMEM((side // 16, 16, RAYS), jnp.bfloat16),
            pltpu.VMEM((GROUP, RAYS, RAYS), jnp.float32),
            pltpu.VMEM((GROUP, RAYS, RAYS), jnp.float32),
            pltpu.VMEM((4, RAYS, RAYS), jnp.float32),
            pltpu.SMEM((groups,), jnp.int32),
            pltpu.SMEM(((RAYS // FRAG) ** 2,), jnp.int32),
        ],
        compiler_params=pltpu.CompilerParams(vmem_limit_bytes=32 * 2**20),
        cost_estimate=pl.CostEstimate(
            flops=2 * SAMPLES * RAYS * side * (side + RAYS),
            bytes_accessed=brick.size * 2,
            transcendentals=6 * SAMPLES * RAYS * RAYS,
        ),
        name="render",
    )(
        brick,
        taps_of(shear_pair[0], side),
        taps_of(shear_pair[1], side),
        scalars,
        rows_live,
        target,
        perm,
        owner,
    )


def over(front, back):
    veil = 1.0 - front[3:4]
    return jnp.concatenate([front[:3] + veil * back[:3], front[3:4] + veil * back[3:4]], 0)


def compose_kernel(
    outgoing,
    slots,
    view,
    owner,
    result,
    got,
    got_slots,
    slot_of,
    layer,
    given,
    taken,
    send_sem,
    recv_sem,
    note_send,
    note_recv,
    local_sem,
    swap_send,
    swap_recv,
    join_send,
    join_recv,
):
    groups = owner.shape[0]
    slabs = lax.axis_size("depth")
    levels = slabs.bit_length() - 1
    column = lax.axis_index("tile")
    slab = lax.axis_index("depth")
    mesh_id = pl.DeviceIdType.MESH

    def bit(level):
        return (slab // 2**level) % 2

    def partner(level):
        return (column, slab + 2**level * (1 - 2 * bit(level)))

    barrier = pltpu.get_barrier_semaphore()
    for j in range(1, groups):
        there = (lax.rem(column + j, groups), slab)
        pl.semaphore_signal(barrier, inc=1, device_id=there, device_id_type=mesh_id)
    for level in range(levels):
        pl.semaphore_signal(barrier, inc=1, device_id=partner(level), device_id_type=mesh_id)
    pl.semaphore_wait(barrier, groups - 1 + levels)

    def note_copy(j, source):
        peer = lax.rem(column + j, groups)
        return pltpu.make_async_remote_copy(
            src_ref=slots.at[peer],
            dst_ref=got_slots.at[source],
            send_sem=note_send.at[j],
            recv_sem=note_recv.at[source],
            device_id=(peer, slab),
            device_id_type=mesh_id,
        )

    def frag_copy(j, source):
        peer = lax.rem(column + j, groups)
        return pltpu.make_async_remote_copy(
            src_ref=outgoing.at[pl.ds(peer * CAP, CAP)],
            dst_ref=got.at[pl.ds(source * CAP, CAP)],
            send_sem=send_sem.at[j],
            recv_sem=recv_sem.at[source],
            device_id=(peer, slab),
            device_id_type=mesh_id,
        )

    for j in range(1, groups):
        note_copy(j, column).start()
    for j in range(1, groups):
        frag_copy(j, column).start()
    own_note = pltpu.make_async_copy(slots.at[column], got_slots.at[column], local_sem.at[0])
    own_frags = pltpu.make_async_copy(
        outgoing.at[pl.ds(column * CAP, CAP)], got.at[pl.ds(column * CAP, CAP)], local_sem.at[1]
    )
    own_note.start()
    own_frags.start()
    own_note.wait()
    for j in range(1, groups):
        note_copy(j, lax.rem(column + groups - j, groups)).wait()
    to_scalar = pltpu.make_async_copy(got_slots, slot_of, local_sem.at[2])
    to_scalar.start()
    to_scalar.wait()
    own_frags.wait()
    for j in range(1, groups):
        frag_copy(j, lax.rem(column + groups - j, groups)).wait()

    mine_view = jnp.int32(0)
    for t in range(groups):
        mine_view = jnp.where(owner[t] == column, view[t], mine_view)

    low = lax.broadcasted_iota(jnp.int32, (FRAG, 2 * FRAG), 1) < FRAG
    per_tile = TILE_SIDE // FRAG

    def landed(position):
        def one(source, total):
            slot = slot_of[source, 0, position]
            block = got[source * CAP + jnp.maximum(slot, 0)].astype(jnp.float32)
            return total + jnp.where(slot >= 0, block, 0.0)

        total = jnp.zeros((2, FRAG, 2 * FRAG), jnp.float32)
        if groups <= 4:
            for source in range(groups):
                total = one(source, total)
            return total
        return lax.fori_loop(0, groups, one, total)

    def lay(frag_row, store):
        for pair in range(per_tile // 2):
            left = landed(frag_row * per_tile + 2 * pair)
            right = landed(frag_row * per_tile + 2 * pair + 1)
            lanes = slice(pair * 2 * FRAG, (pair + 1) * 2 * FRAG)
            for c in range(2):
                store(2 * c, lanes, jnp.where(low, left[c], pltpu.roll(right[c], FRAG, 1)))
                store(2 * c + 1, lanes, jnp.where(low, pltpu.roll(left[c], FRAG, 1), right[c]))

    half = TILE_SIDE // 2
    rows_in_half = half // FRAG

    def lay_given(step, carry):
        def store(channel, lanes, value):
            given[channel, pl.ds(step * FRAG, FRAG), lanes] = value.astype(jnp.bfloat16)

        lay((1 - bit(0)) * rows_in_half + step, store)
        return carry

    def lay_kept(step, carry):
        def store(channel, lanes, value):
            layer[channel, pl.ds(step * FRAG, FRAG), lanes] = value

        lay(bit(0) * rows_in_half + step, store)
        return carry

    def swap(level, height, at):
        return pltpu.make_async_remote_copy(
            src_ref=given.at[:, pl.ds(at, height)],
            dst_ref=taken.at[:, pl.ds(at, height)],
            send_sem=swap_send.at[level],
            recv_sem=swap_recv.at[level],
            device_id=partner(level),
            device_id_type=mesh_id,
        )

    lax.fori_loop(0, rows_in_half, lay_given, 0)
    first = swap(0, half, 0)
    first.start()
    lax.fori_loop(0, rows_in_half, lay_kept, 0)

    chunk = 16
    copy = first
    height = half
    at = 0
    start = 0
    offset = bit(0) * half
    for level in range(levels):
        copy.wait()
        mine_front = (bit(level) + mine_view) % 2 == 0
        last = level == levels - 1

        def blend(from_row, count, put, mine_front=mine_front, at=at, start=start):
            def step(index, carry):
                row = pl.multiple_of(from_row + index * chunk, chunk)
                mine = layer[:, pl.ds(start + row, chunk)]
                other = taken[:, pl.ds(at + row, chunk)].astype(jnp.float32)
                front = jnp.where(mine_front, mine, other)
                back = jnp.where(mine_front, other, mine)
                put(pl.multiple_of(index * chunk, chunk), over(front, back))
                return carry

            lax.fori_loop(0, count // chunk, step, 0)

        if last:

            def put_result(row, value, offset=offset):
                result[:, pl.ds(pl.multiple_of(offset + row, chunk), chunk)] = value.astype(
                    jnp.bfloat16
                )

            blend(0, height, put_result)
        else:
            lower = height // 2
            after = at + height

            def put_given(row, value, after=after):
                given[:, pl.ds(pl.multiple_of(after + row, chunk), chunk)] = value.astype(
                    jnp.bfloat16
                )

            def put_kept(row, value, base=half * 2 - height):
                layer[:, pl.ds(pl.multiple_of(base + row, chunk), chunk)] = value

            blend((1 - bit(level + 1)) * lower, lower, put_given)
            copy = swap(level + 1, lower, after)
            copy.start()
            blend(bit(level + 1) * lower, lower, put_kept)
            start = half * 2 - height
            offset = offset + bit(level + 1) * lower
            at = after
            height = lower

    for level in reversed(range(levels)):
        rows = pl.ds(pl.multiple_of(offset, chunk), height)
        join = pltpu.make_async_remote_copy(
            src_ref=result.at[:, rows],
            dst_ref=result.at[:, rows],
            send_sem=join_send.at[level],
            recv_sem=join_recv.at[level],
            device_id=partner(level),
            device_id_type=mesh_id,
        )
        join.start()
        join.wait()
        offset = offset - bit(level) * height
        height = height * 2


def compose(outgoing, slots, tile_view, tile_owner):
    groups = tile_owner.shape[0]
    levels = lax.axis_size("depth").bit_length() - 1
    smem = pl.BlockSpec(memory_space=pltpu.SMEM)
    vmem = pl.BlockSpec(memory_space=pltpu.VMEM)
    dma = pltpu.SemaphoreType.DMA
    return pl.pallas_call(
        compose_kernel,
        out_shape=jax.ShapeDtypeStruct((4, TILE_SIDE, TILE_SIDE), jnp.bfloat16),
        in_specs=[vmem, vmem, smem, smem],
        out_specs=vmem,
        scratch_shapes=[
            pltpu.VMEM(outgoing.shape, jnp.bfloat16),
            pltpu.VMEM(slots.shape, jnp.int32),
            pltpu.SMEM(slots.shape, jnp.int32),
            pltpu.VMEM((4, TILE_SIDE, TILE_SIDE), jnp.float32),
            pltpu.VMEM((4, TILE_SIDE, TILE_SIDE), jnp.bfloat16),
            pltpu.VMEM((4, TILE_SIDE, TILE_SIDE), jnp.bfloat16),
            dma((groups,)),
            dma((groups,)),
            dma((groups,)),
            dma((groups,)),
            dma((3,)),
            dma((levels,)),
            dma((levels,)),
            dma((levels,)),
            dma((levels,)),
        ],
        compiler_params=pltpu.CompilerParams(
            collective_id=0, has_side_effects=True, vmem_limit_bytes=32 * 2**20
        ),
        cost_estimate=pl.CostEstimate(
            flops=2**24, bytes_accessed=2 * outgoing.size, transcendentals=0
        ),
        name="compose",
    )(outgoing, slots, tile_view, tile_owner)


def local(
    volume,
    shear,
    absorb,
    color_slope,
    color_bias,
    frag_tile,
    slot_perm,
    frag_rows,
    tile_view,
    tile_owner,
):
    outgoing, slots = render(
        volume[0, 0],
        shear[0, 0],
        absorb[0, 0],
        color_slope,
        color_bias,
        frag_rows[0, 0],
        frag_tile[0, 0, :, 0],
        slot_perm[0, 0].reshape(-1),
        tile_owner,
    )
    return compose(outgoing, slots, tile_view, tile_owner)[None]


def solution(mesh):
    in_specs = (
        P("tile", "depth", None, None, None),
        P("tile", "depth", None),
        P("tile", "depth"),
        P(),
        P(),
        P("tile", "depth", None, None),
        P("tile", "depth", None, None),
        P("tile", "depth", None),
        P(),
        P(),
    )
    out_specs = P("tile", None, None, None)
    return jax.shard_map(local, mesh=mesh, in_specs=in_specs, out_specs=out_specs, check_vma=False)
```

```python
import functools
import jax
import jax.numpy as jnp
from jax import lax
from jax.experimental import pallas as pl
from jax.experimental.pallas import tpu as pltpu
from jax.sharding import PartitionSpec as P

SAMPLES = 128
RAYS = 256
FRAG = 64
TILE_SIDE = 256
CAP = 4
POS = 16
GROUP = 4
ROWS = 16
TAPS = 4
LOG2E = 1.4426950408889634


def spline(offset):
    size_abs = jnp.abs(offset)
    inner = 2.0 / 3.0 - size_abs * size_abs + 0.5 * size_abs * size_abs * size_abs
    remain = 2.0 - size_abs
    outer = remain * remain * remain / 6.0
    return jnp.where(size_abs < 1.0, inner, jnp.where(size_abs < 2.0, outer, 0.0))


def taps_of(shear, side):
    per = RAYS // side
    shape = (SAMPLES, 128)
    sample = lax.broadcasted_iota(jnp.int32, shape, 0).astype(jnp.float32)
    lane = lax.broadcasted_iota(jnp.int32, shape, 1)
    parity = ((lane // (2 * TAPS)) % per).astype(jnp.float32)
    reach = (lane % TAPS).astype(jnp.float32) - 1.0
    base = (parity + 0.5) / per - 0.5
    shift = jnp.where((lane // (2 * TAPS * per)) % 2 == 0, shear[0, 0, 0], shear[0, 0, 1])
    place = base + shift * (sample - (side - 1) / 2.0)
    whole = jnp.floor(place)
    weight = spline(place - whole - reach)
    return jnp.where((lane // TAPS) % 2 == 0, weight, whole + reach)


def band(taps, sample, at, offsets, odd):
    def value(index):
        even_one = taps[sample, at + index]
        odd_one = taps[sample, at + 2 * TAPS + index]
        return jnp.where(odd, odd_one, even_one).astype(jnp.bfloat16)

    result = jnp.zeros(offsets.shape, jnp.bfloat16)
    for tap in range(TAPS):
        result = jnp.where(offsets == value(TAPS + tap)[None], value(tap)[None], result)
    return result


def render_kernel(
    brick,
    shear,
    absorb,
    color_slope,
    color_bias,
    rows_live,
    target,
    perm,
    owner,
    outgoing,
    slots,
    row_off,
    col_off,
    field_a,
    field_b,
    state,
    dealt,
    place,
    volume,
    taps_wide,
    taps,
    copy_sem,
):
    side = brick.shape[2]
    head = 4 * GROUP
    bring_head = pltpu.make_async_copy(
        brick.at[0, 0, pl.ds(0, head)], volume.at[pl.ds(0, head)], copy_sem.at[0]
    )
    bring_rest = pltpu.make_async_copy(
        brick.at[0, 0, pl.ds(head, side - head)],
        volume.at[pl.ds(head, side - head)],
        copy_sem.at[1],
    )
    bring_head.start()
    bring_rest.start()
    taps_wide[...] = taps_of(shear, side)
    bring_taps = pltpu.make_async_copy(taps_wide, taps, copy_sem.at[2])
    bring_taps.start()
    per = RAYS // side
    first = jnp.float32(jnp.bfloat16(2.0 / 3.0))
    second = jnp.float32(jnp.bfloat16(1.0 / 6.0))
    fade = absorb[0, 0] * -LOG2E
    slope = [color_slope[k] * 0.5 for k in range(3)]
    bias = [color_bias[k] * 0.5 for k in range(3)]

    row_shape = (RAYS // 16, 16, side)
    ray = lax.broadcasted_iota(jnp.int32, row_shape, 0) * 16 + lax.broadcasted_iota(
        jnp.int32, row_shape, 1
    )
    cell = lax.broadcasted_iota(jnp.int32, row_shape, 2)
    row_off[...] = (cell - ray // per).astype(jnp.float32).astype(jnp.bfloat16)
    col_shape = (side // 16, 16, RAYS)
    cell = lax.broadcasted_iota(jnp.int32, col_shape, 0) * 16 + lax.broadcasted_iota(
        jnp.int32, col_shape, 1
    )
    ray = lax.broadcasted_iota(jnp.int32, col_shape, 2)
    col_off[...] = (cell - ray // per).astype(jnp.float32).astype(jnp.bfloat16)
    row_odd = lax.broadcasted_iota(jnp.int32, (16, side), 0) % per == 1
    col_odd = lax.broadcasted_iota(jnp.int32, (16, RAYS), 1) % per == 1

    state[0] = jnp.ones((RAYS, RAYS), jnp.float32)
    for k in range(3):
        state[1 + k] = jnp.zeros((RAYS, RAYS), jnp.float32)

    def fields(start, out):
        last = SAMPLES - 1
        slices = [
            volume[jnp.clip(start + j - 1, 0, last)].astype(jnp.float32) for j in range(GROUP + 2)
        ]
        for j in range(GROUP):
            sample = jnp.minimum(start + j, last)
            below = jnp.where(sample == 0, 0.0, second)
            above = jnp.where(sample == last, 0.0, second)
            part = slices[j] * below + slices[j + 1] * first + slices[j + 2] * above
            part = part.astype(jnp.bfloat16)
            row_table = band(taps, sample, 0, row_off[...], row_odd).reshape(RAYS, side)
            col_table = band(taps, sample, 2 * TAPS * per, col_off[...], col_odd).reshape(side, RAYS)
            half_way = jnp.dot(row_table, part, preferred_element_type=jnp.float32)
            out[j] = jnp.dot(
                half_way.astype(jnp.bfloat16), col_table, preferred_element_type=jnp.float32
            )

    def integrate(source):
        for tile in range(RAYS // ROWS):
            rows = slice(tile * ROWS, (tile + 1) * ROWS)
            clear = state[0, rows]
            colors = [state[1 + k, rows] for k in range(3)]
            for j in range(GROUP):
                field = source[j, rows]
                soft = jnp.log(1.0 + jnp.exp2(field * LOG2E))
                after = clear * jnp.exp2(soft * fade)
                weight = clear - after
                clear = after
                colors = [
                    colors[k] + weight * jnp.tanh(field * slope[k] + bias[k]) for k in range(3)
                ]
            state[0, rows] = clear
            for k in range(3):
                state[1 + k, rows] = colors[k]

    bring_taps.wait()
    bring_head.wait()
    fields(0, field_a)

    def step(index, carry):
        start = index * (2 * GROUP)

        @pl.when(index == 1)
        def rest_is_here():
            bring_rest.wait()

        fields(start + GROUP, field_b)
        integrate(field_a)
        fields(start + 2 * GROUP, field_a)
        integrate(field_b)
        return carry

    lax.fori_loop(0, SAMPLES // (2 * GROUP), step, 0)

    groups = owner.shape[0]
    per_side = RAYS // FRAG
    count = per_side * per_side
    for t in range(groups):
        dealt[t] = 0
        for p in range(POS):
            slots[t, 0, p] = -1
    for f in range(count):
        tile = target[0, 0, f, 0]
        rank = dealt[tile]
        dealt[tile] = rank + 1
        receiver = owner[tile]
        slots[receiver, 0, perm[0, 0, tile, rank]] = rank
        place[f] = receiver * CAP + rank
    if groups * CAP > count:
        outgoing[...] = jnp.zeros(outgoing.shape, outgoing.dtype)

    row = lax.broadcasted_iota(jnp.int32, (FRAG, 2 * FRAG), 0)
    low = lax.broadcasted_iota(jnp.int32, (FRAG, 2 * FRAG), 1) < FRAG
    for fu in range(per_side):
        for pair in range(per_side // 2):
            f = fu * per_side + 2 * pair
            keep = row < jnp.where(low, rows_live[0, 0, f], rows_live[0, 0, f + 1])
            rows = slice(fu * FRAG, (fu + 1) * FRAG)
            lanes = slice(pair * 2 * FRAG, (pair + 1) * 2 * FRAG)
            alpha = 1.0 - state[0, rows, lanes]
            parts = [0.5 * (alpha + state[1 + k, rows, lanes]) for k in range(3)] + [alpha]
            parts = [jnp.where(keep, part, 0.0) for part in parts]
            turned = [pltpu.roll(part, FRAG, 1) for part in parts]
            for c in range(2):
                even = jnp.where(low, parts[2 * c], turned[2 * c + 1])
                odd = jnp.where(low, turned[2 * c], parts[2 * c + 1])
                outgoing[place[f], c] = even.astype(jnp.bfloat16)
                outgoing[place[f + 1], c] = odd.astype(jnp.bfloat16)


def render(brick, shear, absorb, color_slope, color_bias, rows_live, target, perm, owner):
    side = brick.shape[2]
    groups = owner.shape[0]
    smem = pl.BlockSpec(memory_space=pltpu.SMEM)
    vmem = pl.BlockSpec(memory_space=pltpu.VMEM)
    return pl.pallas_call(
        render_kernel,
        out_shape=(
            jax.ShapeDtypeStruct((groups * CAP, 2, FRAG, 2 * FRAG), jnp.bfloat16),
            jax.ShapeDtypeStruct((groups, 8, 128), jnp.int32),
        ),
        in_specs=[pl.BlockSpec(memory_space=pl.ANY)] + [smem] * 8,
        out_specs=(vmem, smem),
        scratch_shapes=[
            pltpu.VMEM((RAYS // 16, 16, side), jnp.bfloat16),
            pltpu.VMEM((side // 16, 16, RAYS), jnp.bfloat16),
            pltpu.VMEM((GROUP, RAYS, RAYS), jnp.float32),
            pltpu.VMEM((GROUP, RAYS, RAYS), jnp.float32),
            pltpu.VMEM((4, RAYS, RAYS), jnp.float32),
            pltpu.SMEM((groups,), jnp.int32),
            pltpu.SMEM(((RAYS // FRAG) ** 2,), jnp.int32),
            pltpu.VMEM((side, side, side), jnp.bfloat16),
            pltpu.VMEM((SAMPLES, 128), jnp.float32),
            pltpu.SMEM((SAMPLES, 128), jnp.float32),
            pltpu.SemaphoreType.DMA((3,)),
        ],
        compiler_params=pltpu.CompilerParams(vmem_limit_bytes=56 * 2**20),
        cost_estimate=pl.CostEstimate(
            flops=2 * SAMPLES * RAYS * side * (side + RAYS),
            bytes_accessed=brick.size * 2,
            transcendentals=6 * SAMPLES * RAYS * RAYS,
        ),
        name="render",
    )(brick, shear, absorb, color_slope, color_bias, rows_live, target, perm, owner)


def over(front, back):
    veil = 1.0 - front[3:4]
    return jnp.concatenate([front[:3] + veil * back[:3], front[3:4] + veil * back[3:4]], 0)


def compose_kernel(
    outgoing,
    slots,
    view,
    owner,
    result,
    got_first,
    got_second,
    got_slots,
    slot_of,
    layer,
    given,
    taken,
    send_sem,
    recv_sem,
    note_send,
    note_recv,
    local_sem,
    swap_send,
    swap_recv,
    join_send,
    join_recv,
):
    groups = owner.shape[0]
    slabs = lax.axis_size("depth")
    levels = slabs.bit_length() - 1
    column = lax.axis_index("tile")
    slab = lax.axis_index("depth")
    mesh_id = pl.DeviceIdType.MESH

    def bit(level):
        return (slab // 2**level) % 2

    def partner(level):
        return (column, slab + 2**level * (1 - 2 * bit(level)))

    barrier = pltpu.get_barrier_semaphore()
    for j in range(1, groups):
        there = (lax.rem(column + j, groups), slab)
        pl.semaphore_signal(barrier, inc=1, device_id=there, device_id_type=mesh_id)
    for level in range(levels):
        pl.semaphore_signal(barrier, inc=1, device_id=partner(level), device_id_type=mesh_id)
    pl.semaphore_wait(barrier, groups - 1 + levels)

    def note_copy(j, source):
        peer = lax.rem(column + j, groups)
        return pltpu.make_async_remote_copy(
            src_ref=slots.at[peer],
            dst_ref=got_slots.at[source],
            send_sem=note_send.at[j],
            recv_sem=note_recv.at[source],
            device_id=(peer, slab),
            device_id_type=mesh_id,
        )

    chunks = given.shape[0]
    got = (got_first, got_second)
    part = FRAG // chunks
    rows_all = TILE_SIDE // chunks

    def frag_copy(chunk, j, source):
        peer = lax.rem(column + j, groups)
        rows = pl.ds(chunk * part, part)
        return pltpu.make_async_remote_copy(
            src_ref=outgoing.at[pl.ds(peer * CAP, CAP), :, rows],
            dst_ref=got[chunk].at[pl.ds(source * CAP, CAP)],
            send_sem=send_sem.at[chunk, j],
            recv_sem=recv_sem.at[chunk, source],
            device_id=(peer, slab),
            device_id_type=mesh_id,
        )

    for j in range(1, groups):
        note_copy(j, column).start()
    for chunk in range(chunks):
        for j in range(1, groups):
            frag_copy(chunk, j, column).start()
    own_note = pltpu.make_async_copy(slots.at[column], got_slots.at[column], local_sem.at[0])
    own_frags = [
        pltpu.make_async_copy(
            outgoing.at[pl.ds(column * CAP, CAP), :, pl.ds(chunk * part, part)],
            got[chunk].at[pl.ds(column * CAP, CAP)],
            local_sem.at[2 + chunk],
        )
        for chunk in range(chunks)
    ]
    own_note.start()
    for own in own_frags:
        own.start()
    own_note.wait()
    for j in range(1, groups):
        note_copy(j, lax.rem(column + groups - j, groups)).wait()
    to_scalar = pltpu.make_async_copy(got_slots, slot_of, local_sem.at[1])
    to_scalar.start()
    to_scalar.wait()
    for own in own_frags:
        own.wait()

    mine_view = jnp.int32(0)
    for t in range(groups):
        mine_view = jnp.where(owner[t] == column, view[t], mine_view)

    low = lax.broadcasted_iota(jnp.int32, (part, 2 * FRAG), 1) < FRAG
    per_tile = TILE_SIDE // FRAG
    block = 16

    def landed(chunk, position):
        def one(source, total):
            slot = slot_of[source, 0, position]
            index = source * CAP + jnp.maximum(slot, 0)
            found = got[chunk][index].astype(jnp.float32)
            return total + jnp.where(slot >= 0, found, 0.0)

        total = jnp.zeros((2, part, 2 * FRAG), jnp.float32)
        if groups <= 4:
            for source in range(groups):
                total = one(source, total)
            return total
        return lax.fori_loop(0, groups, one, total)

    def lay(chunk, frag_row, store):
        for pair in range(per_tile // 2):
            left = landed(chunk, frag_row * per_tile + 2 * pair)
            right = landed(chunk, frag_row * per_tile + 2 * pair + 1)
            lanes = slice(pair * 2 * FRAG, (pair + 1) * 2 * FRAG)
            for c in range(2):
                store(2 * c, lanes, jnp.where(low, left[c], pltpu.roll(right[c], FRAG, 1)))
                store(2 * c + 1, lanes, jnp.where(low, pltpu.roll(left[c], FRAG, 1), right[c]))

    half = rows_all // 2
    frag_rows_half = per_tile // 2

    def swap(chunk, level, height, at):
        return pltpu.make_async_remote_copy(
            src_ref=given.at[chunk, :, pl.ds(at, height)],
            dst_ref=taken.at[chunk, :, pl.ds(at, height)],
            send_sem=swap_send.at[chunk, level],
            recv_sem=swap_recv.at[chunk, level],
            device_id=partner(level),
            device_id_type=mesh_id,
        )

    def spot(chunk, offset, height):
        if height >= part:
            return (
                slice(None),
                pl.ds(lax.div(offset, part), height // part),
                pl.ds(chunk * part, part),
            )
        row = pl.multiple_of(chunk * part + lax.rem(offset, part), block)
        return (slice(None), pl.ds(lax.div(offset, part), 1), pl.ds(row, height))

    def steps(chunk):
        for j in range(1, groups):
            frag_copy(chunk, j, lax.rem(column + groups - j, groups)).wait()

        def lay_given(step, carry):
            def store(channel, lanes, value):
                rows = pl.ds(pl.multiple_of(step * part, part), part)
                given[chunk, channel, rows, lanes] = value.astype(jnp.bfloat16)

            lay(chunk, (1 - bit(0)) * frag_rows_half + step, store)
            return carry

        def lay_kept(step, carry):
            def store(channel, lanes, value):
                rows = pl.ds(pl.multiple_of(step * part, part), part)
                layer[chunk, channel, rows, lanes] = value

            lay(chunk, bit(0) * frag_rows_half + step, store)
            return carry

        lax.fori_loop(0, frag_rows_half, lay_given, 0)
        copy = swap(chunk, 0, half, 0)
        copy.start()
        lax.fori_loop(0, frag_rows_half, lay_kept, 0)
        yield

        height = half
        at = 0
        start = 0
        offset = bit(0) * half
        for level in range(levels):
            copy.wait()
            mine_front = (bit(level) + mine_view) % 2 == 0

            def blend(from_row, count, put, mine_front=mine_front, at=at, start=start):
                def step(index, carry):
                    row = pl.multiple_of(from_row + index * block, block)
                    mine = layer[chunk, :, pl.ds(start + row, block)]
                    other = taken[chunk, :, pl.ds(at + row, block)].astype(jnp.float32)
                    front = jnp.where(mine_front, mine, other)
                    back = jnp.where(mine_front, other, mine)
                    put(pl.multiple_of(index * block, block), over(front, back))
                    return carry

                lax.fori_loop(0, count // block, step, 0)

            if level == levels - 1:

                def put_result(row, value, offset=offset):
                    where = spot(chunk, offset + row, block)
                    result[where] = value.astype(jnp.bfloat16)[:, None]

                blend(0, height, put_result)
                break
            lower = height // 2
            after = at + height
            below = rows_all - height

            def put_given(row, value, after=after):
                rows = pl.ds(pl.multiple_of(after + row, block), block)
                given[chunk, :, rows] = value.astype(jnp.bfloat16)

            def put_kept(row, value, below=below):
                layer[chunk, :, pl.ds(pl.multiple_of(below + row, block), block)] = value

            blend((1 - bit(level + 1)) * lower, lower, put_given)
            copy = swap(chunk, level + 1, lower, after)
            copy.start()
            blend(bit(level + 1) * lower, lower, put_kept)
            yield
            start = below
            offset = offset + bit(level + 1) * lower
            at = after
            height = lower

        for level in reversed(range(levels)):
            where = spot(chunk, offset, height)
            join = pltpu.make_async_remote_copy(
                src_ref=result.at[where],
                dst_ref=result.at[where],
                send_sem=join_send.at[chunk, level],
                recv_sem=join_recv.at[chunk, level],
                device_id=partner(level),
                device_id_type=mesh_id,
            )
            join.start()
            yield
            join.wait()
            offset = offset - bit(level) * height
            height = height * 2

    running = [steps(chunk) for chunk in range(chunks)]
    while running:
        running = [one for one in running if next(one, "done") != "done"]


def compose(outgoing, slots, tile_view, tile_owner):
    groups = tile_owner.shape[0]
    slabs = lax.axis_size("depth")
    levels = slabs.bit_length() - 1
    chunks = max(1, min(2, TILE_SIDE // (16 * slabs)))
    per_tile = TILE_SIDE // FRAG
    rows = TILE_SIDE // chunks
    smem = pl.BlockSpec(memory_space=pltpu.SMEM)
    vmem = pl.BlockSpec(memory_space=pltpu.VMEM)
    dma = pltpu.SemaphoreType.DMA
    return pl.pallas_call(
        compose_kernel,
        out_shape=jax.ShapeDtypeStruct((4, per_tile, FRAG, TILE_SIDE), jnp.bfloat16),
        in_specs=[vmem, vmem, smem, smem],
        out_specs=vmem,
        scratch_shapes=[
            pltpu.VMEM((groups * CAP, 2, FRAG // chunks, 2 * FRAG), jnp.bfloat16),
            pltpu.VMEM((groups * CAP, 2, FRAG // chunks, 2 * FRAG), jnp.bfloat16),
            pltpu.VMEM(slots.shape, jnp.int32),
            pltpu.SMEM(slots.shape, jnp.int32),
            pltpu.VMEM((chunks, 4, rows, TILE_SIDE), jnp.float32),
            pltpu.VMEM((chunks, 4, rows, TILE_SIDE), jnp.bfloat16),
            pltpu.VMEM((chunks, 4, rows, TILE_SIDE), jnp.bfloat16),
            dma((chunks, groups)),
            dma((chunks, groups)),
            dma((groups,)),
            dma((groups,)),
            dma((4,)),
            dma((chunks, levels)),
            dma((chunks, levels)),
            dma((chunks, levels)),
            dma((chunks, levels)),
        ],
        compiler_params=pltpu.CompilerParams(
            collective_id=0, has_side_effects=True, vmem_limit_bytes=32 * 2**20
        ),
        cost_estimate=pl.CostEstimate(
            flops=2**24, bytes_accessed=2 * outgoing.size, transcendentals=0
        ),
        name="compose",
    )(outgoing, slots, tile_view, tile_owner)


def local(
    volume,
    shear,
    absorb,
    color_slope,
    color_bias,
    frag_tile,
    slot_perm,
    frag_rows,
    tile_view,
    tile_owner,
):
    outgoing, slots = render(
        volume,
        shear,
        absorb,
        color_slope,
        color_bias,
        frag_rows,
        frag_tile,
        slot_perm,
        tile_owner,
    )
    frame = compose(outgoing, slots, tile_view, tile_owner)
    return frame.reshape(1, 4, TILE_SIDE, TILE_SIDE)


def solution(mesh):
    in_specs = (
        P("tile", "depth", None, None, None),
        P("tile", "depth", None),
        P("tile", "depth"),
        P(),
        P(),
        P("tile", "depth", None, None),
        P("tile", "depth", None, None),
        P("tile", "depth", None),
        P(),
        P(),
    )
    out_specs = P("tile", None, None, None)
    return jax.shard_map(local, mesh=mesh, in_specs=in_specs, out_specs=out_specs, check_vma=False)
```

```python
import functools
import jax
import jax.numpy as jnp
from jax import lax
from jax.experimental import pallas as pl
from jax.experimental.pallas import tpu as pltpu
from jax.sharding import PartitionSpec as P

SAMPLES = 128
RAYS = 256
FRAG = 64
TILE_SIDE = 256
CAP = 4
POS = 16
GROUP = 4
ROWS = 16
TAPS = 4
LOG2E = 1.4426950408889634


def spline(offset):
    size_abs = jnp.abs(offset)
    inner = 2.0 / 3.0 - size_abs * size_abs + 0.5 * size_abs * size_abs * size_abs
    remain = 2.0 - size_abs
    outer = remain * remain * remain / 6.0
    return jnp.where(size_abs < 1.0, inner, jnp.where(size_abs < 2.0, outer, 0.0))


def taps_of(shear, side):
    per = RAYS // side
    shape = (SAMPLES, 128)
    sample = lax.broadcasted_iota(jnp.int32, shape, 0).astype(jnp.float32)
    lane = lax.broadcasted_iota(jnp.int32, shape, 1)
    parity = ((lane // (2 * TAPS)) % per).astype(jnp.float32)
    reach = (lane % TAPS).astype(jnp.float32) - 1.0
    base = (parity + 0.5) / per - 0.5
    shift = jnp.where((lane // (2 * TAPS * per)) % 2 == 0, shear[0, 0, 0], shear[0, 0, 1])
    place = base + shift * (sample - (side - 1) / 2.0)
    whole = jnp.floor(place)
    weight = spline(place - whole - reach)
    return jnp.where((lane // TAPS) % 2 == 0, weight, whole + reach)


def band(taps, sample, at, offsets, odd):
    def value(index):
        even_one = taps[sample, at + index]
        odd_one = taps[sample, at + 2 * TAPS + index]
        return jnp.where(odd, odd_one, even_one).astype(jnp.bfloat16)

    result = jnp.zeros(offsets.shape, jnp.bfloat16)
    for tap in range(TAPS):
        result = jnp.where(offsets == value(TAPS + tap)[None], value(tap)[None], result)
    return result


def render_kernel(
    brick,
    shear,
    absorb,
    color_slope,
    color_bias,
    rows_live,
    target,
    perm,
    owner,
    outgoing,
    slots,
    row_off,
    col_off,
    field_a,
    field_b,
    state,
    dealt,
    place,
    volume,
    taps_wide,
    taps,
    copy_sem,
):
    side = brick.shape[2]
    head = 4 * GROUP
    bring_head = pltpu.make_async_copy(
        brick.at[0, 0, pl.ds(0, head)], volume.at[pl.ds(0, head)], copy_sem.at[0]
    )
    bring_rest = pltpu.make_async_copy(
        brick.at[0, 0, pl.ds(head, side - head)],
        volume.at[pl.ds(head, side - head)],
        copy_sem.at[1],
    )
    bring_head.start()
    bring_rest.start()
    taps_wide[...] = taps_of(shear, side)
    bring_taps = pltpu.make_async_copy(taps_wide, taps, copy_sem.at[2])
    bring_taps.start()
    per = RAYS // side
    first = jnp.float32(jnp.bfloat16(2.0 / 3.0))
    second = jnp.float32(jnp.bfloat16(1.0 / 6.0))
    fade = absorb[0, 0] * -LOG2E
    slope = [color_slope[k] * 0.5 for k in range(3)]
    bias = [color_bias[k] * 0.5 for k in range(3)]

    row_shape = (RAYS // 16, 16, side)
    ray = lax.broadcasted_iota(jnp.int32, row_shape, 0) * 16 + lax.broadcasted_iota(
        jnp.int32, row_shape, 1
    )
    cell = lax.broadcasted_iota(jnp.int32, row_shape, 2)
    row_off[...] = (cell - ray // per).astype(jnp.float32).astype(jnp.bfloat16)
    col_shape = (side // 16, 16, RAYS)
    cell = lax.broadcasted_iota(jnp.int32, col_shape, 0) * 16 + lax.broadcasted_iota(
        jnp.int32, col_shape, 1
    )
    ray = lax.broadcasted_iota(jnp.int32, col_shape, 2)
    col_off[...] = (cell - ray // per).astype(jnp.float32).astype(jnp.bfloat16)
    row_odd = lax.broadcasted_iota(jnp.int32, (16, side), 0) % per == 1
    col_odd = lax.broadcasted_iota(jnp.int32, (16, RAYS), 1) % per == 1

    state[0] = jnp.ones((RAYS, RAYS), jnp.float32)
    for k in range(3):
        state[1 + k] = jnp.zeros((RAYS, RAYS), jnp.float32)

    def fields(start, out):
        last = SAMPLES - 1
        slices = [
            volume[jnp.clip(start + j - 1, 0, last)].astype(jnp.float32) for j in range(GROUP + 2)
        ]
        for j in range(GROUP):
            sample = jnp.minimum(start + j, last)
            below = jnp.where(sample == 0, 0.0, second)
            above = jnp.where(sample == last, 0.0, second)
            part = slices[j] * below + slices[j + 1] * first + slices[j + 2] * above
            part = part.astype(jnp.bfloat16)
            row_table = band(taps, sample, 0, row_off[...], row_odd).reshape(RAYS, side)
            col_table = band(taps, sample, 2 * TAPS * per, col_off[...], col_odd).reshape(side, RAYS)
            half_way = jnp.dot(row_table, part, preferred_element_type=jnp.float32)
            yield
            out[j] = jnp.dot(
                half_way.astype(jnp.bfloat16), col_table, preferred_element_type=jnp.float32
            )
            yield

    def integrate(source):
        for tile in range(RAYS // ROWS):
            rows = slice(tile * ROWS, (tile + 1) * ROWS)
            clear = state[0, rows]
            colors = [state[1 + k, rows] for k in range(3)]
            for j in range(GROUP):
                field = source[j, rows]
                soft = jnp.log(1.0 + jnp.exp2(field * LOG2E))
                after = clear * jnp.exp2(soft * fade)
                weight = clear - after
                clear = after
                colors = [
                    colors[k] + weight * jnp.tanh(field * slope[k] + bias[k]) for k in range(3)
                ]
            state[0, rows] = clear
            for k in range(3):
                state[1 + k, rows] = colors[k]
            yield

    def both(making, using):
        share = RAYS // ROWS // (2 * GROUP)
        for unused in making:
            for tile in range(share):
                next(using, None)
        for unused in using:
            pass

    bring_taps.wait()
    bring_head.wait()
    for unused in fields(0, field_a):
        pass

    def step(index, carry):
        start = index * (2 * GROUP)

        @pl.when(index == 1)
        def rest_is_here():
            bring_rest.wait()

        both(fields(start + GROUP, field_b), integrate(field_a))
        both(fields(start + 2 * GROUP, field_a), integrate(field_b))
        return carry

    lax.fori_loop(0, SAMPLES // (2 * GROUP), step, 0)

    groups = owner.shape[0]
    per_side = RAYS // FRAG
    count = per_side * per_side
    for t in range(groups):
        dealt[t] = 0
        for p in range(POS):
            slots[t, 0, p] = -1
    for f in range(count):
        tile = target[f]
        rank = dealt[tile]
        dealt[tile] = rank + 1
        receiver = owner[tile]
        slots[receiver, 0, perm[0, 0, tile, rank]] = rank
        place[f] = receiver * CAP + rank
    if groups * CAP > count:
        outgoing[...] = jnp.zeros(outgoing.shape, outgoing.dtype)

    row = lax.broadcasted_iota(jnp.int32, (FRAG, 2 * FRAG), 0)
    low = lax.broadcasted_iota(jnp.int32, (FRAG, 2 * FRAG), 1) < FRAG
    for fu in range(per_side):
        for pair in range(per_side // 2):
            f = fu * per_side + 2 * pair
            keep = row < jnp.where(low, rows_live[0, 0, f], rows_live[0, 0, f + 1])
            rows = slice(fu * FRAG, (fu + 1) * FRAG)
            lanes = slice(pair * 2 * FRAG, (pair + 1) * 2 * FRAG)
            alpha = 1.0 - state[0, rows, lanes]
            parts = [0.5 * (alpha + state[1 + k, rows, lanes]) for k in range(3)] + [alpha]
            parts = [jnp.where(keep, part, 0.0) for part in parts]
            turned = [pltpu.roll(part, FRAG, 1) for part in parts]
            for c in range(2):
                even = jnp.where(low, parts[2 * c], turned[2 * c + 1])
                odd = jnp.where(low, turned[2 * c], parts[2 * c + 1])
                outgoing[place[f], c] = even.astype(jnp.bfloat16)
                outgoing[place[f + 1], c] = odd.astype(jnp.bfloat16)


def render(brick, shear, absorb, color_slope, color_bias, rows_live, target, perm, owner):
    side = brick.shape[2]
    groups = owner.shape[0]
    smem = pl.BlockSpec(memory_space=pltpu.SMEM)
    vmem = pl.BlockSpec(memory_space=pltpu.VMEM)
    return pl.pallas_call(
        render_kernel,
        out_shape=(
            jax.ShapeDtypeStruct((groups * CAP, 2, FRAG, 2 * FRAG), jnp.bfloat16),
            jax.ShapeDtypeStruct((groups, 8, 128), jnp.int32),
        ),
        in_specs=[pl.BlockSpec(memory_space=pl.ANY)] + [smem] * 8,
        out_specs=(vmem, smem),
        scratch_shapes=[
            pltpu.VMEM((RAYS // 16, 16, side), jnp.bfloat16),
            pltpu.VMEM((side // 16, 16, RAYS), jnp.bfloat16),
            pltpu.VMEM((GROUP, RAYS, RAYS), jnp.float32),
            pltpu.VMEM((GROUP, RAYS, RAYS), jnp.float32),
            pltpu.VMEM((4, RAYS, RAYS), jnp.float32),
            pltpu.SMEM((groups,), jnp.int32),
            pltpu.SMEM(((RAYS // FRAG) ** 2,), jnp.int32),
            pltpu.VMEM((side, side, side), jnp.bfloat16),
            pltpu.VMEM((SAMPLES, 128), jnp.float32),
            pltpu.SMEM((SAMPLES, 128), jnp.float32),
            pltpu.SemaphoreType.DMA((3,)),
        ],
        compiler_params=pltpu.CompilerParams(vmem_limit_bytes=56 * 2**20),
        cost_estimate=pl.CostEstimate(
            flops=2 * SAMPLES * RAYS * side * (side + RAYS),
            bytes_accessed=brick.size * 2,
            transcendentals=6 * SAMPLES * RAYS * RAYS,
        ),
        name="render",
    )(brick, shear, absorb, color_slope, color_bias, rows_live, target, perm, owner)


def over(front, back):
    veil = 1.0 - front[3:4]
    return jnp.concatenate([front[:3] + veil * back[:3], front[3:4] + veil * back[3:4]], 0)


def compose_kernel(
    outgoing,
    slots,
    view,
    owner,
    result,
    got_first,
    got_second,
    got_slots,
    slot_of,
    layer,
    given,
    taken,
    send_sem,
    recv_sem,
    note_send,
    note_recv,
    local_sem,
    swap_send,
    swap_recv,
    join_send,
    join_recv,
):
    groups = owner.shape[0]
    slabs = lax.axis_size("depth")
    levels = slabs.bit_length() - 1
    column = lax.axis_index("tile")
    slab = lax.axis_index("depth")
    mesh_id = pl.DeviceIdType.MESH

    def bit(level):
        return (slab // 2**level) % 2

    def partner(level):
        return (column, slab + 2**level * (1 - 2 * bit(level)))

    barrier = pltpu.get_barrier_semaphore()
    for j in range(1, groups):
        there = (lax.rem(column + j, groups), slab)
        pl.semaphore_signal(barrier, inc=1, device_id=there, device_id_type=mesh_id)
    for level in range(levels):
        pl.semaphore_signal(barrier, inc=1, device_id=partner(level), device_id_type=mesh_id)
    pl.semaphore_wait(barrier, groups - 1 + levels)

    def note_copy(j, source):
        peer = lax.rem(column + j, groups)
        return pltpu.make_async_remote_copy(
            src_ref=slots.at[peer],
            dst_ref=got_slots.at[source],
            send_sem=note_send.at[j],
            recv_sem=note_recv.at[source],
            device_id=(peer, slab),
            device_id_type=mesh_id,
        )

    chunks = given.shape[0]
    got = (got_first, got_second)
    part = FRAG // chunks
    rows_all = TILE_SIDE // chunks

    def frag_copy(chunk, j, source):
        peer = lax.rem(column + j, groups)
        rows = pl.ds(chunk * part, part)
        return pltpu.make_async_remote_copy(
            src_ref=outgoing.at[pl.ds(peer * CAP, CAP), :, rows],
            dst_ref=got[chunk].at[pl.ds(source * CAP, CAP)],
            send_sem=send_sem.at[chunk, j],
            recv_sem=recv_sem.at[chunk, source],
            device_id=(peer, slab),
            device_id_type=mesh_id,
        )

    for j in range(1, groups):
        note_copy(j, column).start()
    for chunk in range(chunks):
        for j in range(1, groups):
            frag_copy(chunk, j, column).start()
    own_note = pltpu.make_async_copy(slots.at[column], got_slots.at[column], local_sem.at[0])
    own_frags = [
        pltpu.make_async_copy(
            outgoing.at[pl.ds(column * CAP, CAP), :, pl.ds(chunk * part, part)],
            got[chunk].at[pl.ds(column * CAP, CAP)],
            local_sem.at[2 + chunk],
        )
        for chunk in range(chunks)
    ]
    own_note.start()
    for own in own_frags:
        own.start()
    own_note.wait()
    for j in range(1, groups):
        note_copy(j, lax.rem(column + groups - j, groups)).wait()
    to_scalar = pltpu.make_async_copy(got_slots, slot_of, local_sem.at[1])
    to_scalar.start()
    to_scalar.wait()
    for own in own_frags:
        own.wait()

    mine_view = jnp.int32(0)
    for t in range(groups):
        mine_view = jnp.where(owner[t] == column, view[t], mine_view)

    low = lax.broadcasted_iota(jnp.int32, (part, 2 * FRAG), 1) < FRAG
    per_tile = TILE_SIDE // FRAG
    block = 16

    def landed(chunk, position):
        def one(source, total):
            slot = slot_of[source, 0, position]
            index = source * CAP + jnp.maximum(slot, 0)
            found = got[chunk][index].astype(jnp.float32)
            return total + jnp.where(slot >= 0, found, 0.0)

        total = jnp.zeros((2, part, 2 * FRAG), jnp.float32)
        if groups <= 4:
            for source in range(groups):
                total = one(source, total)
            return total
        return lax.fori_loop(0, groups, one, total)

    def lay(chunk, frag_row, store):
        for pair in range(per_tile // 2):
            left = landed(chunk, frag_row * per_tile + 2 * pair)
            right = landed(chunk, frag_row * per_tile + 2 * pair + 1)
            lanes = slice(pair * 2 * FRAG, (pair + 1) * 2 * FRAG)
            for c in range(2):
                store(2 * c, lanes, jnp.where(low, left[c], pltpu.roll(right[c], FRAG, 1)))
                store(2 * c + 1, lanes, jnp.where(low, pltpu.roll(left[c], FRAG, 1), right[c]))

    half = rows_all // 2
    frag_rows_half = per_tile // 2

    def swap(chunk, level, height, at):
        return pltpu.make_async_remote_copy(
            src_ref=given.at[chunk, :, pl.ds(at, height)],
            dst_ref=taken.at[chunk, :, pl.ds(at, height)],
            send_sem=swap_send.at[chunk, level],
            recv_sem=swap_recv.at[chunk, level],
            device_id=partner(level),
            device_id_type=mesh_id,
        )

    def spot(chunk, offset, height):
        if height >= part:
            return (
                slice(None),
                pl.ds(lax.div(offset, part), height // part),
                pl.ds(chunk * part, part),
            )
        row = pl.multiple_of(chunk * part + lax.rem(offset, part), block)
        return (slice(None), pl.ds(lax.div(offset, part), 1), pl.ds(row, height))

    def steps(chunk):
        for j in range(1, groups):
            frag_copy(chunk, j, lax.rem(column + groups - j, groups)).wait()

        def lay_given(step, carry):
            def store(channel, lanes, value):
                rows = pl.ds(pl.multiple_of(step * part, part), part)
                given[chunk, channel, rows, lanes] = value.astype(jnp.bfloat16)

            lay(chunk, (1 - bit(0)) * frag_rows_half + step, store)
            return carry

        def lay_kept(step, carry):
            def store(channel, lanes, value):
                rows = pl.ds(pl.multiple_of(step * part, part), part)
                layer[chunk, channel, rows, lanes] = value

            lay(chunk, bit(0) * frag_rows_half + step, store)
            return carry

        lax.fori_loop(0, frag_rows_half, lay_given, 0)
        copy = swap(chunk, 0, half, 0)
        copy.start()
        lax.fori_loop(0, frag_rows_half, lay_kept, 0)
        yield

        height = half
        at = 0
        start = 0
        offset = bit(0) * half
        for level in range(levels):
            copy.wait()
            mine_front = (bit(level) + mine_view) % 2 == 0

            def blend(from_row, count, put, mine_front=mine_front, at=at, start=start):
                def step(index, carry):
                    row = pl.multiple_of(from_row + index * block, block)
                    mine = layer[chunk, :, pl.ds(start + row, block)]
                    other = taken[chunk, :, pl.ds(at + row, block)].astype(jnp.float32)
                    front = jnp.where(mine_front, mine, other)
                    back = jnp.where(mine_front, other, mine)
                    put(pl.multiple_of(index * block, block), over(front, back))
                    return carry

                lax.fori_loop(0, count // block, step, 0)

            if level == levels - 1:

                def put_result(row, value, offset=offset):
                    where = spot(chunk, offset + row, block)
                    result[where] = value.astype(jnp.bfloat16)[:, None]

                blend(0, height, put_result)
                break
            lower = height // 2
            after = at + height
            below = rows_all - height

            def put_given(row, value, after=after):
                rows = pl.ds(pl.multiple_of(after + row, block), block)
                given[chunk, :, rows] = value.astype(jnp.bfloat16)

            def put_kept(row, value, below=below):
                layer[chunk, :, pl.ds(pl.multiple_of(below + row, block), block)] = value

            blend((1 - bit(level + 1)) * lower, lower, put_given)
            copy = swap(chunk, level + 1, lower, after)
            copy.start()
            blend(bit(level + 1) * lower, lower, put_kept)
            yield
            start = below
            offset = offset + bit(level + 1) * lower
            at = after
            height = lower

        for level in reversed(range(levels)):
            where = spot(chunk, offset, height)
            join = pltpu.make_async_remote_copy(
                src_ref=result.at[where],
                dst_ref=result.at[where],
                send_sem=join_send.at[chunk, level],
                recv_sem=join_recv.at[chunk, level],
                device_id=partner(level),
                device_id_type=mesh_id,
            )
            join.start()
            yield
            join.wait()
            offset = offset - bit(level) * height
            height = height * 2

    running = [steps(chunk) for chunk in range(chunks)]
    while running:
        running = [one for one in running if next(one, "done") != "done"]


def compose(outgoing, slots, tile_view, tile_owner):
    groups = tile_owner.shape[0]
    slabs = lax.axis_size("depth")
    levels = slabs.bit_length() - 1
    chunks = max(1, min(2, TILE_SIDE // (16 * slabs)))
    per_tile = TILE_SIDE // FRAG
    rows = TILE_SIDE // chunks
    smem = pl.BlockSpec(memory_space=pltpu.SMEM)
    vmem = pl.BlockSpec(memory_space=pltpu.VMEM)
    dma = pltpu.SemaphoreType.DMA
    return pl.pallas_call(
        compose_kernel,
        out_shape=jax.ShapeDtypeStruct((4, per_tile, FRAG, TILE_SIDE), jnp.bfloat16),
        in_specs=[pl.BlockSpec(memory_space=pl.ANY)] * 2 + [smem, smem],
        out_specs=vmem,
        scratch_shapes=[
            pltpu.VMEM((groups * CAP, 2, FRAG // chunks, 2 * FRAG), jnp.bfloat16),
            pltpu.VMEM((groups * CAP, 2, FRAG // chunks, 2 * FRAG), jnp.bfloat16),
            pltpu.VMEM(slots.shape, jnp.int32),
            pltpu.SMEM(slots.shape, jnp.int32),
            pltpu.VMEM((chunks, 4, rows, TILE_SIDE), jnp.float32),
            pltpu.VMEM((chunks, 4, rows, TILE_SIDE), jnp.bfloat16),
            pltpu.VMEM((chunks, 4, rows, TILE_SIDE), jnp.bfloat16),
            dma((chunks, groups)),
            dma((chunks, groups)),
            dma((groups,)),
            dma((groups,)),
            dma((4,)),
            dma((chunks, levels)),
            dma((chunks, levels)),
            dma((chunks, levels)),
            dma((chunks, levels)),
        ],
        compiler_params=pltpu.CompilerParams(
            collective_id=0, has_side_effects=True, vmem_limit_bytes=56 * 2**20
        ),
        cost_estimate=pl.CostEstimate(
            flops=2**24, bytes_accessed=2 * outgoing.size, transcendentals=0
        ),
        name="compose",
    )(outgoing, slots, tile_view, tile_owner)


def local(
    volume,
    shear,
    absorb,
    color_slope,
    color_bias,
    frag_tile,
    slot_perm,
    frag_rows,
    tile_view,
    tile_owner,
):
    outgoing, slots = render(
        volume,
        shear,
        absorb,
        color_slope,
        color_bias,
        frag_rows,
        frag_tile[0, 0, :, 0],
        slot_perm,
        tile_owner,
    )
    frame = compose(outgoing, slots, tile_view, tile_owner)
    return frame.reshape(1, 4, TILE_SIDE, TILE_SIDE)


def solution(mesh):
    in_specs = (
        P("tile", "depth", None, None, None),
        P("tile", "depth", None),
        P("tile", "depth"),
        P(),
        P(),
        P("tile", "depth", None, None),
        P("tile", "depth", None, None),
        P("tile", "depth", None),
        P(),
        P(),
    )
    out_specs = P("tile", None, None, None)
    return jax.shard_map(local, mesh=mesh, in_specs=in_specs, out_specs=out_specs, check_vma=False)
```

```python
import functools
import jax
import jax.numpy as jnp
from jax import lax
from jax.experimental import pallas as pl
from jax.experimental.pallas import tpu as pltpu
from jax.sharding import PartitionSpec as P

SAMPLES = 128
RAYS = 256
FRAG = 64
TILE_SIDE = 256
CAP = 4
POS = 16
GROUP = 4
ROWS = 16
TAPS = 4
LOG2E = 1.4426950408889634


def spline(offset):
    size_abs = jnp.abs(offset)
    inner = 2.0 / 3.0 - size_abs * size_abs + 0.5 * size_abs * size_abs * size_abs
    remain = 2.0 - size_abs
    outer = remain * remain * remain / 6.0
    return jnp.where(size_abs < 1.0, inner, jnp.where(size_abs < 2.0, outer, 0.0))


def taps_of(shear, side):
    per = RAYS // side
    shape = (SAMPLES, 128)
    sample = lax.broadcasted_iota(jnp.int32, shape, 0).astype(jnp.float32)
    lane = lax.broadcasted_iota(jnp.int32, shape, 1)
    parity = ((lane // (2 * TAPS)) % per).astype(jnp.float32)
    reach = (lane % TAPS).astype(jnp.float32) - 1.0
    base = (parity + 0.5) / per - 0.5
    shift = jnp.where((lane // (2 * TAPS * per)) % 2 == 0, shear[0, 0, 0], shear[0, 0, 1])
    place = base + shift * (sample - (side - 1) / 2.0)
    whole = jnp.floor(place)
    weight = spline(place - whole - reach)
    return jnp.where((lane // TAPS) % 2 == 0, weight, whole + reach)


def band(taps, sample, at, offsets, odd):
    def value(index):
        even_one = taps[sample, at + index]
        odd_one = taps[sample, at + 2 * TAPS + index]
        return jnp.where(odd, odd_one, even_one).astype(jnp.bfloat16)

    result = jnp.zeros(offsets.shape, jnp.bfloat16)
    for tap in range(TAPS):
        result = jnp.where(offsets == value(TAPS + tap)[None], value(tap)[None], result)
    return result


def render_kernel(
    brick,
    shear,
    absorb,
    color_slope,
    color_bias,
    rows_live,
    target,
    perm,
    owner,
    outgoing,
    slots,
    row_off,
    col_off,
    field_a,
    field_b,
    state,
    dealt,
    place,
    volume,
    taps_wide,
    taps,
    copy_sem,
):
    side = brick.shape[2]
    head = 4 * GROUP
    bring_head = pltpu.make_async_copy(
        brick.at[0, 0, pl.ds(0, head)], volume.at[pl.ds(0, head)], copy_sem.at[0]
    )
    bring_rest = pltpu.make_async_copy(
        brick.at[0, 0, pl.ds(head, side - head)],
        volume.at[pl.ds(head, side - head)],
        copy_sem.at[1],
    )
    bring_head.start()
    bring_rest.start()
    taps_wide[...] = taps_of(shear, side)
    bring_taps = pltpu.make_async_copy(taps_wide, taps, copy_sem.at[2])
    bring_taps.start()
    per = RAYS // side
    first = jnp.float32(jnp.bfloat16(2.0 / 3.0))
    second = jnp.float32(jnp.bfloat16(1.0 / 6.0))
    fade = absorb[0, 0] * -LOG2E
    slope = [color_slope[k] * 0.5 for k in range(3)]
    bias = [color_bias[k] * 0.5 for k in range(3)]

    row_shape = (RAYS // 16, 16, side)
    ray = lax.broadcasted_iota(jnp.int32, row_shape, 0) * 16 + lax.broadcasted_iota(
        jnp.int32, row_shape, 1
    )
    cell = lax.broadcasted_iota(jnp.int32, row_shape, 2)
    row_off[...] = (cell - ray // per).astype(jnp.float32).astype(jnp.bfloat16)
    col_shape = (side // 16, 16, RAYS)
    cell = lax.broadcasted_iota(jnp.int32, col_shape, 0) * 16 + lax.broadcasted_iota(
        jnp.int32, col_shape, 1
    )
    ray = lax.broadcasted_iota(jnp.int32, col_shape, 2)
    col_off[...] = (cell - ray // per).astype(jnp.float32).astype(jnp.bfloat16)
    row_odd = lax.broadcasted_iota(jnp.int32, (16, side), 0) % per == 1
    col_odd = lax.broadcasted_iota(jnp.int32, (16, RAYS), 1) % per == 1

    state[0] = jnp.ones((RAYS, RAYS), jnp.float32)
    for k in range(3):
        state[1 + k] = jnp.zeros((RAYS, RAYS), jnp.float32)

    def fields(start, out):
        last = SAMPLES - 1
        slices = [
            volume[jnp.clip(start + j - 1, 0, last)].astype(jnp.float32) for j in range(GROUP + 2)
        ]
        for j in range(GROUP):
            sample = jnp.minimum(start + j, last)
            below = jnp.where(sample == 0, 0.0, second)
            above = jnp.where(sample == last, 0.0, second)
            part = slices[j] * below + slices[j + 1] * first + slices[j + 2] * above
            part = part.astype(jnp.bfloat16)
            row_table = band(taps, sample, 0, row_off[...], row_odd).reshape(RAYS, side)
            col_table = band(taps, sample, 2 * TAPS * per, col_off[...], col_odd).reshape(side, RAYS)
            half_way = jnp.dot(row_table, part, preferred_element_type=jnp.float32)
            yield
            out[j] = jnp.dot(
                half_way.astype(jnp.bfloat16), col_table, preferred_element_type=jnp.float32
            )
            yield

    def integrate(source):
        for tile in range(RAYS // ROWS):
            rows = slice(tile * ROWS, (tile + 1) * ROWS)
            clear = state[0, rows]
            colors = [state[1 + k, rows] for k in range(3)]
            for j in range(GROUP):
                field = source[j, rows]
                soft = jnp.log(1.0 + jnp.exp2(field * LOG2E))
                after = clear * jnp.exp2(soft * fade)
                weight = clear - after
                clear = after
                turns = [
                    jnp.tanh((field * slope[k] + bias[k]).astype(jnp.bfloat16)) for k in range(3)
                ]
                colors = [
                    colors[k] + weight * turns[k].astype(jnp.float32) for k in range(3)
                ]
            state[0, rows] = clear
            for k in range(3):
                state[1 + k, rows] = colors[k]
            yield

    def both(making, using):
        share = RAYS // ROWS // (2 * GROUP)
        for unused in making:
            for tile in range(share):
                next(using, None)
        for unused in using:
            pass

    bring_taps.wait()
    bring_head.wait()
    for unused in fields(0, field_a):
        pass

    def step(index, carry):
        start = index * (2 * GROUP)

        @pl.when(index == 1)
        def rest_is_here():
            bring_rest.wait()

        both(fields(start + GROUP, field_b), integrate(field_a))
        both(fields(start + 2 * GROUP, field_a), integrate(field_b))
        return carry

    lax.fori_loop(0, SAMPLES // (2 * GROUP), step, 0)

    groups = owner.shape[0]
    per_side = RAYS // FRAG
    count = per_side * per_side
    for t in range(groups):
        dealt[t] = 0
        for p in range(POS):
            slots[t, 0, p] = -1
    for f in range(count):
        tile = target[f]
        rank = dealt[tile]
        dealt[tile] = rank + 1
        receiver = owner[tile]
        slots[receiver, 0, perm[0, 0, tile, rank]] = rank
        place[f] = receiver * CAP + rank
    if groups * CAP > count:
        outgoing[...] = jnp.zeros(outgoing.shape, outgoing.dtype)

    row = lax.broadcasted_iota(jnp.int32, (FRAG, 2 * FRAG), 0)
    low = lax.broadcasted_iota(jnp.int32, (FRAG, 2 * FRAG), 1) < FRAG
    for fu in range(per_side):
        for pair in range(per_side // 2):
            f = fu * per_side + 2 * pair
            keep = row < jnp.where(low, rows_live[0, 0, f], rows_live[0, 0, f + 1])
            rows = slice(fu * FRAG, (fu + 1) * FRAG)
            lanes = slice(pair * 2 * FRAG, (pair + 1) * 2 * FRAG)
            alpha = 1.0 - state[0, rows, lanes]
            parts = [0.5 * (alpha + state[1 + k, rows, lanes]) for k in range(3)] + [alpha]
            parts = [jnp.where(keep, part, 0.0) for part in parts]
            turned = [pltpu.roll(part, FRAG, 1) for part in parts]
            for c in range(2):
                even = jnp.where(low, parts[2 * c], turned[2 * c + 1])
                odd = jnp.where(low, turned[2 * c], parts[2 * c + 1])
                outgoing[place[f], c] = even.astype(jnp.bfloat16)
                outgoing[place[f + 1], c] = odd.astype(jnp.bfloat16)


def render(brick, shear, absorb, color_slope, color_bias, rows_live, target, perm, owner):
    side = brick.shape[2]
    groups = owner.shape[0]
    smem = pl.BlockSpec(memory_space=pltpu.SMEM)
    vmem = pl.BlockSpec(memory_space=pltpu.VMEM)
    return pl.pallas_call(
        render_kernel,
        out_shape=(
            jax.ShapeDtypeStruct((groups * CAP, 2, FRAG, 2 * FRAG), jnp.bfloat16),
            jax.ShapeDtypeStruct((groups, 8, 128), jnp.int32),
        ),
        in_specs=[pl.BlockSpec(memory_space=pl.ANY)] + [smem] * 8,
        out_specs=(vmem, smem),
        scratch_shapes=[
            pltpu.VMEM((RAYS // 16, 16, side), jnp.bfloat16),
            pltpu.VMEM((side // 16, 16, RAYS), jnp.bfloat16),
            pltpu.VMEM((GROUP, RAYS, RAYS), jnp.float32),
            pltpu.VMEM((GROUP, RAYS, RAYS), jnp.float32),
            pltpu.VMEM((4, RAYS, RAYS), jnp.float32),
            pltpu.SMEM((groups,), jnp.int32),
            pltpu.SMEM(((RAYS // FRAG) ** 2,), jnp.int32),
            pltpu.VMEM((side, side, side), jnp.bfloat16),
            pltpu.VMEM((SAMPLES, 128), jnp.float32),
            pltpu.SMEM((SAMPLES, 128), jnp.float32),
            pltpu.SemaphoreType.DMA((3,)),
        ],
        compiler_params=pltpu.CompilerParams(vmem_limit_bytes=56 * 2**20),
        cost_estimate=pl.CostEstimate(
            flops=2 * SAMPLES * RAYS * side * (side + RAYS),
            bytes_accessed=brick.size * 2,
            transcendentals=6 * SAMPLES * RAYS * RAYS,
        ),
        name="render",
    )(brick, shear, absorb, color_slope, color_bias, rows_live, target, perm, owner)


def over(front, back):
    veil = 1.0 - front[3:4]
    return jnp.concatenate([front[:3] + veil * back[:3], front[3:4] + veil * back[3:4]], 0)


def compose_kernel(
    outgoing,
    slots,
    view,
    owner,
    result,
    got_first,
    got_second,
    got_slots,
    slot_of,
    layer,
    given,
    taken,
    send_sem,
    recv_sem,
    note_send,
    note_recv,
    local_sem,
    swap_send,
    swap_recv,
    join_send,
    join_recv,
):
    groups = owner.shape[0]
    slabs = lax.axis_size("depth")
    levels = slabs.bit_length() - 1
    column = lax.axis_index("tile")
    slab = lax.axis_index("depth")
    mesh_id = pl.DeviceIdType.MESH

    def bit(level):
        return (slab // 2**level) % 2

    def partner(level):
        return (column, slab + 2**level * (1 - 2 * bit(level)))

    barrier = pltpu.get_barrier_semaphore()
    for j in range(1, groups):
        there = (lax.rem(column + j, groups), slab)
        pl.semaphore_signal(barrier, inc=1, device_id=there, device_id_type=mesh_id)
    for level in range(levels):
        pl.semaphore_signal(barrier, inc=1, device_id=partner(level), device_id_type=mesh_id)
    pl.semaphore_wait(barrier, groups - 1 + levels)

    def note_copy(j, source):
        peer = lax.rem(column + j, groups)
        return pltpu.make_async_remote_copy(
            src_ref=slots.at[peer],
            dst_ref=got_slots.at[source],
            send_sem=note_send.at[j],
            recv_sem=note_recv.at[source],
            device_id=(peer, slab),
            device_id_type=mesh_id,
        )

    chunks = given.shape[0]
    got = (got_first, got_second)
    part = FRAG // chunks
    rows_all = TILE_SIDE // chunks

    def frag_copy(chunk, j, source):
        peer = lax.rem(column + j, groups)
        rows = pl.ds(chunk * part, part)
        return pltpu.make_async_remote_copy(
            src_ref=outgoing.at[pl.ds(peer * CAP, CAP), :, rows],
            dst_ref=got[chunk].at[pl.ds(source * CAP, CAP)],
            send_sem=send_sem.at[chunk, j],
            recv_sem=recv_sem.at[chunk, source],
            device_id=(peer, slab),
            device_id_type=mesh_id,
        )

    for j in range(1, groups):
        note_copy(j, column).start()
    for chunk in range(chunks):
        for j in range(1, groups):
            frag_copy(chunk, j, column).start()
    own_note = pltpu.make_async_copy(slots.at[column], got_slots.at[column], local_sem.at[0])
    own_frags = [
        pltpu.make_async_copy(
            outgoing.at[pl.ds(column * CAP, CAP), :, pl.ds(chunk * part, part)],
            got[chunk].at[pl.ds(column * CAP, CAP)],
            local_sem.at[2 + chunk],
        )
        for chunk in range(chunks)
    ]
    own_note.start()
    for own in own_frags:
        own.start()
    own_note.wait()
    for j in range(1, groups):
        note_copy(j, lax.rem(column + groups - j, groups)).wait()
    to_scalar = pltpu.make_async_copy(got_slots, slot_of, local_sem.at[1])
    to_scalar.start()
    to_scalar.wait()
    for own in own_frags:
        own.wait()

    mine_view = jnp.int32(0)
    for t in range(groups):
        mine_view = jnp.where(owner[t] == column, view[t], mine_view)

    low = lax.broadcasted_iota(jnp.int32, (part, 2 * FRAG), 1) < FRAG
    per_tile = TILE_SIDE // FRAG
    block = 16

    def landed(chunk, position):
        def one(source, total):
            slot = slot_of[source, 0, position]
            index = source * CAP + jnp.maximum(slot, 0)
            found = got[chunk][index].astype(jnp.float32)
            return total + jnp.where(slot >= 0, found, 0.0)

        total = jnp.zeros((2, part, 2 * FRAG), jnp.float32)
        if groups <= 4:
            for source in range(groups):
                total = one(source, total)
            return total
        return lax.fori_loop(0, groups, one, total)

    def lay(chunk, frag_row, store):
        for pair in range(per_tile // 2):
            left = landed(chunk, frag_row * per_tile + 2 * pair)
            right = landed(chunk, frag_row * per_tile + 2 * pair + 1)
            lanes = slice(pair * 2 * FRAG, (pair + 1) * 2 * FRAG)
            for c in range(2):
                store(2 * c, lanes, jnp.where(low, left[c], pltpu.roll(right[c], FRAG, 1)))
                store(2 * c + 1, lanes, jnp.where(low, pltpu.roll(left[c], FRAG, 1), right[c]))

    half = rows_all // 2
    frag_rows_half = per_tile // 2

    def swap(chunk, level, height, at):
        return pltpu.make_async_remote_copy(
            src_ref=given.at[chunk, :, pl.ds(at, height)],
            dst_ref=taken.at[chunk, :, pl.ds(at, height)],
            send_sem=swap_send.at[chunk, level],
            recv_sem=swap_recv.at[chunk, level],
            device_id=partner(level),
            device_id_type=mesh_id,
        )

    def spot(chunk, offset, height):
        if height >= part:
            return (
                slice(None),
                pl.ds(lax.div(offset, part), height // part),
                pl.ds(chunk * part, part),
            )
        row = pl.multiple_of(chunk * part + lax.rem(offset, part), block)
        return (slice(None), pl.ds(lax.div(offset, part), 1), pl.ds(row, height))

    def steps(chunk):
        for j in range(1, groups):
            frag_copy(chunk, j, lax.rem(column + groups - j, groups)).wait()

        def lay_given(step, carry):
            def store(channel, lanes, value):
                rows = pl.ds(pl.multiple_of(step * part, part), part)
                given[chunk, channel, rows, lanes] = value.astype(jnp.bfloat16)

            lay(chunk, (1 - bit(0)) * frag_rows_half + step, store)
            return carry

        def lay_kept(step, carry):
            def store(channel, lanes, value):
                rows = pl.ds(pl.multiple_of(step * part, part), part)
                layer[chunk, channel, rows, lanes] = value

            lay(chunk, bit(0) * frag_rows_half + step, store)
            return carry

        lax.fori_loop(0, frag_rows_half, lay_given, 0)
        copy = swap(chunk, 0, half, 0)
        copy.start()
        lax.fori_loop(0, frag_rows_half, lay_kept, 0)
        yield

        height = half
        at = 0
        start = 0
        offset = bit(0) * half
        for level in range(levels):
            copy.wait()
            mine_front = (bit(level) + mine_view) % 2 == 0

            def blend(from_row, count, put, mine_front=mine_front, at=at, start=start):
                def step(index, carry):
                    row = pl.multiple_of(from_row + index * block, block)
                    mine = layer[chunk, :, pl.ds(start + row, block)]
                    other = taken[chunk, :, pl.ds(at + row, block)].astype(jnp.float32)
                    front = jnp.where(mine_front, mine, other)
                    back = jnp.where(mine_front, other, mine)
                    put(pl.multiple_of(index * block, block), over(front, back))
                    return carry

                lax.fori_loop(0, count // block, step, 0)

            if level == levels - 1:

                def put_result(row, value, offset=offset):
                    where = spot(chunk, offset + row, block)
                    result[where] = value.astype(jnp.bfloat16)[:, None]

                blend(0, height, put_result)
                break
            lower = height // 2
            after = at + height
            below = rows_all - height

            def put_given(row, value, after=after):
                rows = pl.ds(pl.multiple_of(after + row, block), block)
                given[chunk, :, rows] = value.astype(jnp.bfloat16)

            def put_kept(row, value, below=below):
                layer[chunk, :, pl.ds(pl.multiple_of(below + row, block), block)] = value

            blend((1 - bit(level + 1)) * lower, lower, put_given)
            copy = swap(chunk, level + 1, lower, after)
            copy.start()
            blend(bit(level + 1) * lower, lower, put_kept)
            yield
            start = below
            offset = offset + bit(level + 1) * lower
            at = after
            height = lower

        for level in reversed(range(levels)):
            where = spot(chunk, offset, height)
            join = pltpu.make_async_remote_copy(
                src_ref=result.at[where],
                dst_ref=result.at[where],
                send_sem=join_send.at[chunk, level],
                recv_sem=join_recv.at[chunk, level],
                device_id=partner(level),
                device_id_type=mesh_id,
            )
            join.start()
            yield
            join.wait()
            offset = offset - bit(level) * height
            height = height * 2

    running = [steps(chunk) for chunk in range(chunks)]
    while running:
        running = [one for one in running if next(one, "done") != "done"]


def compose(outgoing, slots, tile_view, tile_owner):
    groups = tile_owner.shape[0]
    slabs = lax.axis_size("depth")
    levels = slabs.bit_length() - 1
    chunks = max(1, min(2, TILE_SIDE // (16 * slabs)))
    per_tile = TILE_SIDE // FRAG
    rows = TILE_SIDE // chunks
    smem = pl.BlockSpec(memory_space=pltpu.SMEM)
    vmem = pl.BlockSpec(memory_space=pltpu.VMEM)
    dma = pltpu.SemaphoreType.DMA
    return pl.pallas_call(
        compose_kernel,
        out_shape=jax.ShapeDtypeStruct((4, per_tile, FRAG, TILE_SIDE), jnp.bfloat16),
        in_specs=[pl.BlockSpec(memory_space=pltpu.HBM)] * 2 + [smem, smem],
        out_specs=vmem,
        scratch_shapes=[
            pltpu.VMEM((groups * CAP, 2, FRAG // chunks, 2 * FRAG), jnp.bfloat16),
            pltpu.VMEM((groups * CAP, 2, FRAG // chunks, 2 * FRAG), jnp.bfloat16),
            pltpu.VMEM(slots.shape, jnp.int32),
            pltpu.SMEM(slots.shape, jnp.int32),
            pltpu.VMEM((chunks, 4, rows, TILE_SIDE), jnp.float32),
            pltpu.VMEM((chunks, 4, rows, TILE_SIDE), jnp.bfloat16),
            pltpu.VMEM((chunks, 4, rows, TILE_SIDE), jnp.bfloat16),
            dma((chunks, groups)),
            dma((chunks, groups)),
            dma((groups,)),
            dma((groups,)),
            dma((4,)),
            dma((chunks, levels)),
            dma((chunks, levels)),
            dma((chunks, levels)),
            dma((chunks, levels)),
        ],
        compiler_params=pltpu.CompilerParams(
            collective_id=0, has_side_effects=True, vmem_limit_bytes=32 * 2**20
        ),
        cost_estimate=pl.CostEstimate(
            flops=2**24, bytes_accessed=2 * outgoing.size, transcendentals=0
        ),
        name="compose",
    )(outgoing, slots, tile_view, tile_owner)


def local(
    volume,
    shear,
    absorb,
    color_slope,
    color_bias,
    frag_tile,
    slot_perm,
    frag_rows,
    tile_view,
    tile_owner,
):
    outgoing, slots = render(
        volume,
        shear,
        absorb,
        color_slope,
        color_bias,
        frag_rows,
        frag_tile[0, 0, :, 0],
        slot_perm,
        tile_owner,
    )
    frame = compose(outgoing, slots, tile_view, tile_owner)
    return frame.reshape(1, 4, TILE_SIDE, TILE_SIDE)


def solution(mesh):
    in_specs = (
        P("tile", "depth", None, None, None),
        P("tile", "depth", None),
        P("tile", "depth"),
        P(),
        P(),
        P("tile", "depth", None, None),
        P("tile", "depth", None, None),
        P("tile", "depth", None),
        P(),
        P(),
    )
    out_specs = P("tile", None, None, None)
    return jax.shard_map(local, mesh=mesh, in_specs=in_specs, out_specs=out_specs, check_vma=False)
```
